512 devices in a mesh: dp: 16 (over x, y), mp: 32 (over z, core).
Axes of the slice: x: 4, y: 4, z: 16, core: 2. Of those that a mesh axis runs over, the one named last changes fastest.
Arguments:
- gradients: bfloat16 [16, 32, 7168, 128], P('dp', None, 'mp'), may hold values from -6 to 6
- owners: int32 [32], replicated, may hold values from 0 to 31, as said below
- momentum: bfloat16 [64, 32, 224, 128], P('mp', None, 'dp'), may hold values from -8 to 8
- master: float32 [64, 32, 224, 128], P('mp', None, 'dp'), may hold values from -0.06 to 0.06
Outputs:
- weights: bfloat16 [32, 7168, 128], P(None, 'mp')
- scales: float32 [32], replicated
- new_momentum: bfloat16 [64, 32, 224, 128], P('mp', None, 'dp')
- new_master: float32 [64, 32, 224, 128], P('mp', None, 'dp')
The draws below stay inside these ranges and needn't reach their ends.
Inputs may be any that keep to these rules, and one draw needn't show every extreme that they name: `owners`: no index of mp owns more than 2 blocks, and one owns exactly 2.
All inputs are finite; a program needn't handle non-finite values.
Results may differ from the reference program's by a relative error of at most 0.009.
Values may be sent and summed in bfloat16 or wider, within the bound.
A program may use at most 64 MiB of HBM per device.

```python
import math
import jax
import jax.numpy as jnp
from jax import lax

D = 7168
HD = 128
ITERS = 5
BLOCKS = 32
CAP = 2
SLOTS = 64
MP_ROWS = 224
N_DP = 16
N_MP = 32


def draw_owners(key, part):
    key = jax.random.fold_in(key, 11)
    key_busy, key_places, key_order = jax.random.split(key, 3)
    busiest = jax.random.randint(key_busy, (), 0, N_MP)
    places = jax.random.permutation(key_places, (N_MP - 1) * CAP)[:BLOCKS - CAP] // CAP
    others = jnp.where(places >= busiest, places + 1, places)
    listed = jnp.concatenate([jnp.full((CAP,), busiest), others]).astype(jnp.int32)
    return jax.random.permutation(key_order, listed)


def with_spikes(result, rng, source, target, blocks, factor):
    owner, partner = [(jnp.arange(result.shape[axis_at]) // (result.shape[axis_at] // blocks)).reshape([-1 if axis == axis_at else 1 for axis in range(result.ndim)]) for axis_at in (source, target)]
    chosen = jax.random.permutation(rng, blocks)[partner]
    strong = (owner == chosen) | (owner == (partner + blocks // 2) % blocks)
    return jnp.where(strong, factor * result, result)


def levels(key, dims, cuts, smallest, high):
    def one(axis_at, shards_of):
        draws = jax.random.uniform(jax.random.fold_in(jax.random.fold_in(key, 6), axis_at), (shards_of,), jnp.float32, smallest / len(cuts), high / len(cuts))
        return jnp.repeat(jnp.exp(draws), dims[axis_at] // shards_of).reshape((-1,) + (1,) * (len(dims) - axis_at - 1))

    level = one(*cuts[0])
    for cut in cuts[1:]:
        level = level * one(*cut)
    return level


def scatter_about(key, dims, width, bound, shards=(), kind=jnp.bfloat16):
    entries = width * jax.random.normal(key, dims, jnp.float32)
    if shards:
        entries = entries * levels(key, dims, shards, -0.22, 0.18)
    return jnp.clip(entries, -bound, bound).astype(kind)


def gaussian_with(stream_key, extent, scale, bound, cuts, heavy, held_as=jnp.bfloat16):
    result = scale * jax.random.normal(stream_key, extent, jnp.float32)
    if cuts:
        result = result * levels(stream_key, extent, cuts, -0.22, 0.18)
    return jnp.clip(with_spikes(result, jax.random.fold_in(stream_key, 3), *heavy), -bound, bound).astype(held_as)


def setup_inputs(seed: int = 0) -> dict:
    keys = jax.random.split(jax.random.key(seed), 5)
    gradients = gaussian_with(keys[0], (N_DP, BLOCKS, D, HD), 1.0, 6.0, ((0, 16), (2, 32)), (0, 2, 16, 2.0))
    owners = draw_owners(jax.random.fold_in(keys[4], 71), 0)
    momentum = scatter_about(keys[2], (SLOTS, N_MP, MP_ROWS, HD), 2.0, 8.0, ((0, 32), (2, 16)))
    master = scatter_about(keys[3], (SLOTS, N_MP, MP_ROWS, HD), 0.01, 0.06, ((0, 32), (2, 16)), jnp.float32)
    return {"gradients": gradients, "owners": owners, "momentum": momentum, "master": master}


NEWTON = (3.4445, -4.775, 2.0315)
decay_rate = 0.95
learn_rate = 0.05
weight_decay = 0.1
update_gain = 0.2

def slot_table(owners):
    number = owners.shape[0]
    same_owner = owners[:, None] == owners[None, :]
    earlier = jnp.arange(number)[None, :] < jnp.arange(number)[:, None]
    return lax.optimization_barrier(jnp.sum(jnp.where(same_owner & earlier, 1, 0), axis=1)).astype(jnp.int32)

def orthogonalize(update):
    raw_gram = jnp.dot(update.T, update, precision=lax.Precision.HIGHEST)
    norm_value = jnp.sqrt(jnp.trace(raw_gram)) + 1e-07
    current = update / norm_value
    gram_now = raw_gram / (norm_value * norm_value)
    for iteration in range(ITERS):
        if iteration > 0:
            gram_now = jnp.dot(current.T, current, precision=lax.Precision.HIGHEST)
        mixing = NEWTON[1] * gram_now + NEWTON[2] * jnp.dot(gram_now, gram_now, precision=lax.Precision.HIGHEST)
        current = NEWTON[0] * current + jnp.dot(current, mixing, precision=lax.Precision.HIGHEST)
    return current

def reference(gradients, owners, momentum, master):

    def accumulate(running, portion):
        return (running + portion.astype(jnp.float32), None)
    summed, _ = lax.scan(accumulate, jnp.zeros(gradients.shape[1:], jnp.float32), gradients)
    position = slot_table(owners)
    slot_ids = (owners * CAP + position).astype(jnp.int32)
    momentum_flat = momentum.reshape(SLOTS, D, HD)
    master_flat = master.reshape(SLOTS, D, HD)
    previous = momentum_flat[slot_ids].astype(jnp.float32)
    momentum_new = (decay_rate * previous + summed).astype(jnp.bfloat16)
    update = summed + decay_rate * momentum_new.astype(jnp.float32)
    old_weights = master_flat[slot_ids]

    def finish(block_pair):
        block_update, block_weight = block_pair
        ortho = orthogonalize(block_update)
        updated = block_weight * (1.0 - learn_rate * weight_decay) - learn_rate * update_gain * math.sqrt(D) * ortho
        peak_value = jnp.max(jnp.abs(updated)) + 1e-06
        return (updated, peak_value)
    new_weights, peak_values = lax.map(finish, (update, old_weights))
    quantized = (new_weights / peak_values[:, None, None]).astype(jnp.bfloat16)
    new_momentum = momentum_flat.at[slot_ids].set(momentum_new).reshape(momentum.shape)
    new_master = master_flat.at[slot_ids].set(new_weights).reshape(master.shape)
    return (quantized, peak_values, new_momentum, new_master)
```

```python
import functools
import math

import jax
import jax.numpy as jnp
from jax import lax
from jax.experimental import pallas as pl
from jax.experimental.pallas import tpu as pltpu
from jax.sharding import PartitionSpec as P

D = 7168
ITERS = 5
NEWTON = (3.4445, -4.775, 2.0315)
decay_rate = 0.95
learn_rate = 0.05
weight_decay = 0.1
update_gain = 0.2

MESH = pl.DeviceIdType.MESH
F32 = jnp.float32
BF16 = jnp.bfloat16
PAD = 16


def dot(a, b):
    return jnp.dot(a, b, precision=lax.Precision.HIGHEST, preferred_element_type=F32)


def kernel(n_dp, n_mp, cap, blocks, rows, owners_ref, grad_ref, mom_ref, master_ref,
           out_ref, scale_ref, newmom_ref, newmaster_ref,
           wide, rs_out, rs_in, z32, z_out, z_in, upd, gram_out, gram_in, gram_all,
           y_out, y_in, ag_out, ag_in,
           rs_s, rs_r, z_s, z_r, g_s, g_r, h_s, h_r, y_s, y_r, ag_s, ag_r):
    dp, mp = lax.axis_index("dp"), lax.axis_index("mp")
    slots = n_mp * cap
    shard = n_dp * rows
    msg = cap * PAD

    def dp_peer(k):
        return lax.rem(dp + k, n_dp), lax.rem(dp + n_dp - k, n_dp)

    def mp_peer(k):
        return lax.rem(mp + k, n_mp), lax.rem(mp + n_mp - k, n_mp)

    barrier = pltpu.get_barrier_semaphore()

    @pl.loop(1, n_dp)
    def _(k):
        pl.semaphore_signal(barrier, 1, device_id={"dp": dp_peer(k)[0]}, device_id_type=MESH)

    @pl.loop(1, n_mp)
    def _(k):
        pl.semaphore_signal(barrier, 1, device_id={"mp": mp_peer(k)[0]}, device_id_type=MESH)

    @pl.loop(0, blocks)
    def _(b):
        at = pl.ds(pl.multiple_of(b * shard, 16), shard)
        wide[at, :] = grad_ref[at, :].astype(F32)

    def pick(d):
        for r in range(rows):
            x = wide[pl.ds(d * rows + r, blocks, stride=shard), :]
            rs_out[d, r] = x.astype(BF16)

    lane = lax.broadcasted_iota(jnp.int32, (8, 128), 1)
    owner_row = jnp.full((8, 128), -1, jnp.int32)
    for b in range(blocks):
        owner_row = jnp.where(lane == b, owners_ref[b], owner_row)
    position = jnp.zeros((8, 128), jnp.int32)
    for b in range(blocks):
        position = position + jnp.where((owner_row == owners_ref[b]) & (lane > b), 1, 0)
    slot_row = jnp.where(owner_row >= 0, owner_row * cap + position, -1)[0:1, 0:blocks]
    place = jnp.broadcast_to(slot_row, (slots, blocks)) == lax.broadcasted_iota(jnp.int32, (slots, blocks), 0)
    onehot = jnp.where(place, 1.0, 0.0).astype(F32)
    onehot_t = onehot.T.astype(BF16)
    onehot = onehot.astype(BF16)
    count = jnp.int32(0)
    for b in range(blocks):
        count = count + jnp.where(owners_ref[b] == mp, 1, 0)

    pl.semaphore_wait(barrier, n_dp + n_mp - 2)

    def rs_copy(k):
        to, _ = dp_peer(k)
        return pltpu.make_async_remote_copy(
            src_ref=rs_out.at[to], dst_ref=rs_in.at[dp], send_sem=rs_s.at[k], recv_sem=rs_r.at[k],
            device_id={"dp": to}, device_id_type=MESH)

    @pl.loop(1, n_dp)
    def _(k):
        pick(dp_peer(k)[0])
        rs_copy(k).start()

    pick(dp)
    rs_in[dp] = rs_out[dp]

    z32[...] = jnp.zeros_like(z32)

    @pl.loop(1, n_dp)
    def _(k):
        _, source = dp_peer(k)
        pltpu.make_async_remote_copy(
            src_ref=rs_out.at[dp], dst_ref=rs_in.at[source], send_sem=rs_s.at[k], recv_sem=rs_r.at[k],
            device_id={"dp": source}, device_id_type=MESH).wait_recv()

    for r in range(rows):
        total = rs_in[0, r].astype(F32)
        for s in range(1, n_dp):
            total = total + rs_in[s, r].astype(F32)
        z32[pl.ds(r, slots, stride=PAD), :] = jnp.dot(onehot, total.astype(BF16), preferred_element_type=F32)

    z_out[...] = z32[...].astype(BF16).reshape(z_out.shape)

    def z_copy(k, src, dst, s, r):
        to, _ = mp_peer(k)
        return pltpu.make_async_remote_copy(
            src_ref=src.at[to], dst_ref=dst.at[mp], send_sem=s.at[k], recv_sem=r.at[k],
            device_id={"mp": to}, device_id_type=MESH)

    def z_wait(k, src, dst, s, r):
        _, source = mp_peer(k)
        pltpu.make_async_remote_copy(
            src_ref=src.at[mp], dst_ref=dst.at[source], send_sem=s.at[k], recv_sem=r.at[k],
            device_id={"mp": source}, device_id_type=MESH).wait_recv()

    @pl.loop(1, n_mp)
    def _(k):
        z_copy(k, z_out, z_in, z_s, z_r).start()

    z_in[mp] = z_out[mp]

    @pl.loop(1, n_mp)
    def _(k):
        z_wait(k, z_out, z_in, z_s, z_r)

    z32[...] = z_in[...].reshape(z32.shape).astype(F32)
    held = n_mp * rows
    for c in range(cap):
        for r in range(rows):
            arrived = z32[pl.ds(c * PAD + r, n_mp, stride=msg), :]
            before = mom_ref[c, r]
            after = (decay_rate * before.astype(F32) + arrived).astype(BF16)
            newmom_ref[c, r] = jnp.where(count > c, after, before)
            upd[c, pl.ds(r * n_mp, n_mp), :] = arrived + decay_rate * after.astype(F32)

    piece = 128 // n_dp
    for c in range(cap):
        u = upd[c]
        gram = lax.dot_general(u, u, (((0,), (0,)), ((), ())), precision=lax.Precision.HIGHEST,
                               preferred_element_type=F32)
        for d in range(n_dp):
            gram_out[d, c] = gram[d * piece:(d + 1) * piece, :]

    @pl.loop(1, n_dp)
    def _(k):
        to, _ = dp_peer(k)
        pltpu.make_async_remote_copy(
            src_ref=gram_out.at[to], dst_ref=gram_in.at[dp], send_sem=g_s.at[k], recv_sem=g_r.at[k],
            device_id={"dp": to}, device_id_type=MESH).start()

    gram_in[dp] = gram_out[dp]

    @pl.loop(1, n_dp)
    def _(k):
        _, source = dp_peer(k)
        pltpu.make_async_remote_copy(
            src_ref=gram_out.at[dp], dst_ref=gram_in.at[source], send_sem=g_s.at[k], recv_sem=g_r.at[k],
            device_id={"dp": source}, device_id_type=MESH).wait_recv()

    part = gram_in[0]
    for s in range(1, n_dp):
        part = part + gram_in[s]
    gram_all[dp] = part

    @pl.loop(1, n_dp)
    def _(k):
        to, _ = dp_peer(k)
        pltpu.make_async_remote_copy(
            src_ref=gram_all.at[dp], dst_ref=gram_all.at[dp], send_sem=h_s.at[k], recv_sem=h_r.at[k],
            device_id={"dp": to}, device_id_type=MESH).start()

    @pl.loop(1, n_dp)
    def _(k):
        _, source = dp_peer(k)
        pltpu.make_async_remote_copy(
            src_ref=gram_all.at[dp], dst_ref=gram_all.at[source], send_sem=h_s.at[k], recv_sem=h_r.at[k],
            device_id={"dp": source}, device_id_type=MESH).wait_recv()

    eye = lax.broadcasted_iota(jnp.int32, (128, 128), 0) == lax.broadcasted_iota(jnp.int32, (128, 128), 1)
    a0, a1, a2 = NEWTON
    grams, polys, norms = [], [], []
    for c in range(cap):
        raw = gram_all[:, c].reshape(128, 128)
        norm = jnp.sqrt(jnp.sum(jnp.where(eye, raw, 0.0), axis=(0, 1), keepdims=True)) + 1e-07
        grams.append(raw / (norm * norm))
        norms.append(norm)
    polys = [None] * cap
    for i in range(ITERS):
        mixes = [a1 * g + a2 * dot(g, g) for g in grams]
        if i == 0:
            polys = [jnp.where(eye, a0, 0.0) + m for m in mixes]
        else:
            polys = [a0 * p + dot(p, m) for p, m in zip(polys, mixes)]
        if i < ITERS - 1:
            halves = [a0 * g + dot(m, g) for g, m in zip(grams, mixes)]
            grams = [a0 * h + dot(h, m) for h, m in zip(halves, mixes)]

    for c in range(cap):
        step = dot(upd[c], polys[c] * (-learn_rate * update_gain * math.sqrt(D) / norms[c]))
        peak = jnp.zeros((n_mp, 128), F32)
        for r in range(rows):
            before = master_ref[c, r]
            after = before * (1.0 - learn_rate * weight_decay) + step[r * n_mp:(r + 1) * n_mp, :]
            newmaster_ref[c, r] = jnp.where(count > c, after, before)
            peak = jnp.maximum(peak, jnp.abs(after))
            z32[pl.ds(c * PAD + r, n_mp, stride=msg), :] = after
        peak = jnp.broadcast_to(jnp.max(peak, axis=(0, 1), keepdims=True), (n_mp, 128))
        high = peak.astype(BF16).astype(F32)
        low = peak - high
        first = lax.broadcasted_iota(jnp.int32, (n_mp, 128), 1) < 64
        z32[pl.ds(c * PAD + rows, n_mp, stride=msg), :] = jnp.where(first, high, low)

    y_out[...] = z32[...].astype(BF16).reshape(y_out.shape)

    @pl.loop(1, n_mp)
    def _(k):
        z_copy(k, y_out, y_in, y_s, y_r).start()

    y_in[mp] = y_out[mp]

    @pl.loop(1, n_mp)
    def _(k):
        z_wait(k, y_out, y_in, y_s, y_r)

    z32[...] = y_in[...].reshape(z32.shape).astype(F32)
    for r in range(rows + 1):
        x = z32[pl.ds(r, slots, stride=PAD), :].astype(BF16)
        ag_out[r] = jnp.dot(onehot_t, x, preferred_element_type=F32).astype(BF16)

    @pl.loop(1, n_dp)
    def _(k):
        to, _ = dp_peer(k)
        pltpu.make_async_remote_copy(
            src_ref=ag_out, dst_ref=ag_in.at[dp], send_sem=ag_s.at[k], recv_sem=ag_r.at[k],
            device_id={"dp": to}, device_id_type=MESH).start()

    ag_in[dp] = ag_out[...]

    def spread(source):
        for r in range(rows):
            wide[pl.ds(source * rows + r, blocks, stride=shard), :] = ag_in[source, r].astype(F32)

    spread(dp)

    @pl.loop(1, n_dp)
    def _(k):
        _, source = dp_peer(k)
        pltpu.make_async_remote_copy(
            src_ref=ag_out, dst_ref=ag_in.at[source], send_sem=ag_s.at[k], recv_sem=ag_r.at[k],
            device_id={"dp": source}, device_id_type=MESH).wait_recv()
        spread(source)

    both = [ag_in[s, rows].astype(F32) for s in range(n_dp)]
    peaks = [x + pltpu.roll(x, 64, 1) for x in both]
    peak = functools.reduce(jnp.maximum, peaks) + 1e-06
    z32[0:blocks, :] = 1.0 / peak
    scale_ref[...] = peak

    @pl.loop(0, blocks)
    def _(b):
        at = pl.ds(pl.multiple_of(b * shard, 16), shard)
        out_ref[at, :] = (wide[at, :] * z32[pl.ds(b, 1), :]).astype(BF16)

    @pl.loop(1, n_dp)
    def _(k):
        rs_copy(k).wait_send()
        for src, s in ((gram_out.at[dp], g_s), (gram_all.at[dp], h_s), (ag_out, ag_s)):
            pltpu.make_async_remote_copy(
                src_ref=src, dst_ref=src, send_sem=s.at[k], recv_sem=s.at[k],
                device_id={"dp": dp_peer(k)[0]}, device_id_type=MESH).wait_send()

    @pl.loop(1, n_mp)
    def _(k):
        z_copy(k, z_out, z_in, z_s, z_r).wait_send()
        z_copy(k, y_out, y_in, y_s, y_r).wait_send()


def body(gradients, owners, momentum, master):
    n_dp, n_mp = lax.axis_size("dp"), lax.axis_size("mp")
    _, blocks, shard, head = gradients.shape
    cap, _, rows, _ = momentum.shape
    slots = n_mp * cap
    msg = cap * PAD
    moved = (cap, rows, n_mp, head)
    sem = pltpu.SemaphoreType.DMA
    vmem = pl.BlockSpec(memory_space=pltpu.VMEM)
    out, scale, newmom, newmaster = pl.pallas_call(
        functools.partial(kernel, n_dp, n_mp, cap, blocks, rows),
        out_shape=(
            jax.ShapeDtypeStruct((blocks * shard, head), BF16),
            jax.ShapeDtypeStruct((blocks, head), F32),
            jax.ShapeDtypeStruct(moved, BF16),
            jax.ShapeDtypeStruct(moved, F32),
        ),
        in_specs=[pl.BlockSpec(memory_space=pltpu.SMEM), vmem, vmem, vmem],
        out_specs=(vmem,) * 4,
        scratch_shapes=[
            pltpu.VMEM((blocks * shard, head), F32),
            pltpu.VMEM((n_dp, rows, blocks, head), BF16),
            pltpu.VMEM((n_dp, rows, blocks, head), BF16),
            pltpu.VMEM((slots * PAD, head), F32),
            pltpu.VMEM((n_mp, msg, head), BF16),
            pltpu.VMEM((n_mp, msg, head), BF16),
            pltpu.VMEM((cap, rows * n_mp, head), F32),
            pltpu.VMEM((n_dp, cap, head // n_dp, head), F32),
            pltpu.VMEM((n_dp, cap, head // n_dp, head), F32),
            pltpu.VMEM((n_dp, cap, head // n_dp, head), F32),
            pltpu.VMEM((n_mp, msg, head), BF16),
            pltpu.VMEM((n_mp, msg, head), BF16),
            pltpu.VMEM((rows + 1, blocks, head), BF16),
            pltpu.VMEM((n_dp, rows + 1, blocks, head), BF16),
            sem((n_dp,)), sem((n_dp,)), sem((n_mp,)), sem((n_mp,)), sem((n_dp,)), sem((n_dp,)),
            sem((n_dp,)), sem((n_dp,)), sem((n_mp,)), sem((n_mp,)), sem((n_dp,)), sem((n_dp,)),
        ],
        compiler_params=pltpu.CompilerParams(
            collective_id=0, has_side_effects=True, vmem_limit_bytes=48 * 2**20),
        name="muon_step",
    )(
        owners,
        gradients.reshape(blocks * shard, head),
        momentum.transpose(0, 2, 1, 3),
        master.transpose(0, 2, 1, 3),
    )
    return (
        out.reshape(blocks, shard, head),
        scale[:, 0],
        newmom.transpose(0, 2, 1, 3),
        newmaster.transpose(0, 2, 1, 3),
    )


def solution(mesh):
    in_specs = (
        P("dp", None, "mp", None),
        P(),
        P("mp", None, "dp", None),
        P("mp", None, "dp", None),
    )
    out_specs = (P(None, "mp", None), P(), P("mp", None, "dp", None), P("mp", None, "dp", None))
    return jax.shard_map(body, mesh=mesh, in_specs=in_specs, out_specs=out_specs, check_vma=False)
```

```python
import functools
import math

import jax
import jax.numpy as jnp
from jax import lax
from jax.experimental import pallas as pl
from jax.experimental.pallas import tpu as pltpu
from jax.sharding import PartitionSpec as P

D = 7168
ITERS = 5
NEWTON = (3.4445, -4.775, 2.0315)
decay_rate = 0.95
learn_rate = 0.05
weight_decay = 0.1
update_gain = 0.2

MESH = pl.DeviceIdType.MESH
F32 = jnp.float32
BF16 = jnp.bfloat16
SIDE = 4


def dot(a, b):
    return jnp.dot(a, b, precision=lax.Precision.HIGHEST, preferred_element_type=F32)


def kernel(n_dp, n_mp, cap, blocks, rows, owners_hbm, grad_hbm, mom_hbm, master_hbm,
           out_ref, scale_ref, newmom_ref, newmaster_ref,
           owners_ref, grad_ref, mom_ref, master_ref, wide,
           rs1_out_a, rs1_out_b, rs1_in_a, rs1_in_b, rs2_out_a, rs2_out_b, rs2_in_a, rs2_in_b,
           z32, z_out, z_in, upd, gram_out, gram_in, gram_all, y_out, y_in, ag_a, ag_b,
           in_sem, rs1_s, rs1_r, rs2_s, rs2_r, z_s, z_r, g_s, g_r, h_s, h_r, y_s, y_r,
           ag1_s, ag1_r, ag2_s, ag2_r):
    dp, mp = lax.axis_index("dp"), lax.axis_index("mp")
    side = SIDE
    x, y = dp // side, lax.rem(dp, side)
    slots = n_mp * cap
    shard = n_dp * rows
    half = blocks // 2
    few, many = 0, 1
    starts, counts = (8, 0), (rows - 8, 8)
    rs1_out, rs1_in = (rs1_out_a, rs1_out_b), (rs1_in_a, rs1_in_b)
    rs2_out, rs2_in = (rs2_out_a, rs2_out_b), (rs2_in_a, rs2_in_b)
    ag = (ag_a, ag_b)
    first, second = (x, y), (y, x)

    def dp_at(h, f, s):
        return f * side + s if h == 0 else s * side + f

    def ahead(v, k, n):
        return lax.rem(v + k, n)

    def behind(v, k, n):
        return lax.rem(v + n - k, n)

    def remote(src, dst, send, recv, **to):
        return pltpu.make_async_remote_copy(
            src_ref=src, dst_ref=dst, send_sem=send, recv_sem=recv, device_id=to, device_id_type=MESH)

    def z_offset(j):
        return n_mp // 2 + ((j + 1) // 2) * (1 - 2 * lax.rem(j, 2))

    loads = [
        pltpu.make_async_copy(src, dst, in_sem.at[i])
        for i, (src, dst) in enumerate((
            (grad_hbm, grad_ref), (owners_hbm, owners_ref), (mom_hbm, mom_ref), (master_hbm, master_ref)))
    ]
    for load in loads:
        load.start()

    barrier = pltpu.get_barrier_semaphore()

    @pl.loop(1, n_dp)
    def _(k):
        pl.semaphore_signal(barrier, 1, device_id={"dp": ahead(dp, k, n_dp)}, device_id_type=MESH)

    @pl.loop(1, n_mp)
    def _(k):
        pl.semaphore_signal(barrier, 1, device_id={"mp": ahead(mp, k, n_mp)}, device_id_type=MESH)

    loads[0].wait()

    @pl.loop(0, blocks)
    def _(b):
        at = pl.ds(pl.multiple_of(b * shard, 16), shard)
        wide[at, :] = grad_ref[at, :].astype(F32)

    def pick(q, h, f, dst):
        @pl.loop(0, side)
        def _(s):
            base = h * half * shard + dp_at(h, f, s) * rows + starts[q]
            for r in range(counts[q]):
                dst[s, r] = wide[pl.ds(base + r, half, stride=shard), :].astype(BF16)

    loads[1].wait()
    lane = lax.broadcasted_iota(jnp.int32, (8, 128), 1)
    owner_row = jnp.full((8, 128), -1, jnp.int32)
    for b in range(blocks):
        owner_row = jnp.where(lane == b, owners_ref[b], owner_row)
    position = jnp.zeros((8, 128), jnp.int32)
    for b in range(blocks):
        position = position + jnp.where((owner_row == owners_ref[b]) & (lane > b), 1, 0)
    slot_row = jnp.where(owner_row >= 0, owner_row * cap + position, -1)[0:1, 0:blocks]
    place = jnp.broadcast_to(slot_row, (slots, blocks)) == lax.broadcasted_iota(jnp.int32, (slots, blocks), 0)
    onehot = jnp.where(place, 1.0, 0.0).astype(F32)
    onehot_t = onehot.T.astype(BF16)
    onehot = onehot.astype(BF16)
    count = jnp.int32(0)
    for b in range(blocks):
        count = count + jnp.where(owners_ref[b] == mp, 1, 0)

    pl.semaphore_wait(barrier, n_dp + n_mp - 2)

    def rs1(q, h, k, f):
        return remote(rs1_out[q].at[h, f], rs1_in[q].at[h, first[h]], rs1_s.at[q, h, k], rs1_r.at[q, h, k],
                      dp=dp_at(h, f, second[h]))

    def rs2(q, h, k, s):
        return remote(rs2_out[q].at[h, s], rs2_in[q].at[h, second[h]], rs2_s.at[q, h, k], rs2_r.at[q, h, k],
                      dp=dp_at(h, first[h], s))

    for q in (few, many):
        for k in range(1, side):
            for h in range(2):
                f = ahead(first[h], k, side)
                pick(q, h, f, rs1_out[q].at[h, f])
                rs1(q, h, k, f).start()
        for h in range(2):
            pick(q, h, first[h], rs1_in[q].at[h, first[h]])

    z32[...] = jnp.zeros_like(z32)

    for q in (few, many):
        for h in range(2):
            for k in range(1, side):
                f = behind(first[h], k, side)
                remote(rs1_out[q].at[h, f], rs1_in[q].at[h, f], rs1_s.at[q, h, k], rs1_r.at[q, h, k],
                       dp=dp_at(h, f, second[h])).wait_recv()
            for k in range(1, side + 1):
                s = ahead(second[h], k, side)
                for r in range(counts[q]):
                    total = rs1_in[q][h, 0, s, r].astype(F32)
                    for f in range(1, side):
                        total = total + rs1_in[q][h, f, s, r].astype(F32)
                    if k < side:
                        rs2_out[q][h, s, r] = total.astype(BF16)
                    else:
                        rs2_in[q][h, s, r] = total.astype(BF16)
                if k < side:
                    rs2(q, h, k, s).start()

    def z_copy(j, q, src, dst, s, r):
        to = ahead(mp, z_offset(j), n_mp)
        return remote(src.at[q, to], dst.at[q, mp], s.at[q, j], r.at[q, j], mp=to)

    def z_send(q, src, dst, s, r):
        @pl.loop(0, n_mp - 1)
        def _(j):
            z_copy(j, q, src, dst, s, r).start()

        dst[q, mp] = src[q, mp]

    def z_wait(q, src, dst, s, r):
        @pl.loop(0, n_mp - 1)
        def _(j):
            source = behind(mp, z_offset(j), n_mp)
            remote(src.at[q, source], dst.at[q, source], s.at[q, j], r.at[q, j], mp=source).wait_recv()

    for q in (few, many):
        for h in range(2):
            for k in range(1, side):
                s = behind(second[h], k, side)
                remote(rs2_out[q].at[h, s], rs2_in[q].at[h, s], rs2_s.at[q, h, k], rs2_r.at[q, h, k],
                       dp=dp_at(h, first[h], s)).wait_recv()
        for r in range(counts[q]):
            both = []
            for h in range(2):
                total = rs2_in[q][h, 0, r].astype(F32)
                for s in range(1, side):
                    total = total + rs2_in[q][h, s, r].astype(F32)
                both.append(total)
            total = jnp.concatenate(both, axis=0).astype(BF16)
            z32[pl.ds(r, slots, stride=8), :] = jnp.dot(onehot, total, preferred_element_type=F32)
        z_out[q] = z32[...].astype(BF16).reshape(n_mp, cap * 8, 128)
        z_send(q, z_out, z_in, z_s, z_r)

    loads[2].wait()
    loads[3].wait()
    for q in (few, many):
        z_wait(q, z_out, z_in, z_s, z_r)
        z32[...] = z_in[q].reshape(z32.shape).astype(F32)
        for c in range(cap):
            for j in range(counts[q]):
                r = starts[q] + j
                arrived = z32[pl.ds(c * 8 + j, n_mp, stride=cap * 8), :]
                before = mom_ref[c, r]
                after = (decay_rate * before.astype(F32) + arrived).astype(BF16)
                newmom_ref[c, r] = jnp.where(count > c, after, before)
                upd[c, pl.ds(r * n_mp, n_mp), :] = arrived + decay_rate * after.astype(F32)

    piece = 128 // n_dp
    for c in range(cap):
        u = upd[c]
        gram = lax.dot_general(u, u, (((0,), (0,)), ((), ())), precision=lax.Precision.HIGHEST,
                               preferred_element_type=F32)
        for d in range(n_dp):
            gram_out[d, c] = gram[d * piece:(d + 1) * piece, :]

    @pl.loop(1, n_dp)
    def _(k):
        to = ahead(dp, k, n_dp)
        remote(gram_out.at[to], gram_in.at[dp], g_s.at[k], g_r.at[k], dp=to).start()

    gram_in[dp] = gram_out[dp]

    @pl.loop(1, n_dp)
    def _(k):
        source = behind(dp, k, n_dp)
        remote(gram_out.at[source], gram_in.at[source], g_s.at[k], g_r.at[k], dp=source).wait_recv()

    part = gram_in[0]
    for s in range(1, n_dp):
        part = part + gram_in[s]
    gram_all[dp] = part

    @pl.loop(1, n_dp)
    def _(k):
        to = ahead(dp, k, n_dp)
        remote(gram_all.at[dp], gram_all.at[dp], h_s.at[k], h_r.at[k], dp=to).start()

    @pl.loop(1, n_dp)
    def _(k):
        source = behind(dp, k, n_dp)
        remote(gram_all.at[source], gram_all.at[source], h_s.at[k], h_r.at[k], dp=source).wait_recv()

    eye = lax.broadcasted_iota(jnp.int32, (128, 128), 0) == lax.broadcasted_iota(jnp.int32, (128, 128), 1)
    a0, a1, a2 = NEWTON
    grams, norms = [], []
    for c in range(cap):
        raw = gram_all[:, c].reshape(128, 128)
        norm = jnp.sqrt(jnp.sum(jnp.where(eye, raw, 0.0), axis=(0, 1), keepdims=True)) + 1e-07
        grams.append(raw / (norm * norm))
        norms.append(norm)
    polys = [None] * cap
    for i in range(ITERS):
        mixes = [a1 * g + a2 * dot(g, g) for g in grams]
        if i == 0:
            polys = [jnp.where(eye, a0, 0.0) + m for m in mixes]
        else:
            polys = [a0 * p + dot(p, m) for p, m in zip(polys, mixes)]
        if i < ITERS - 1:
            halves = [a0 * g + dot(m, g) for g, m in zip(grams, mixes)]
            grams = [a0 * h + dot(h, m) for h, m in zip(halves, mixes)]
    polys = [p * (-learn_rate * update_gain * math.sqrt(D) / n) for p, n in zip(polys, norms)]

    peaks = [jnp.zeros((n_mp, 128), F32)] * cap
    for q in (many, few):
        for c in range(cap):
            at, size = starts[q] * n_mp, counts[q] * n_mp
            step = dot(upd[c, at:at + size, :], polys[c])
            for j in range(counts[q]):
                r = starts[q] + j
                before = master_ref[c, r]
                after = before * (1.0 - learn_rate * weight_decay) + step[j * n_mp:(j + 1) * n_mp, :]
                newmaster_ref[c, r] = jnp.where(count > c, after, before)
                peaks[c] = jnp.maximum(peaks[c], jnp.abs(after))
                z32[pl.ds(c * 8 + j, n_mp, stride=cap * 8), :] = after
            if q == few:
                peak = jnp.broadcast_to(jnp.max(peaks[c], axis=(0, 1), keepdims=True), (n_mp, 128))
                high = peak.astype(BF16).astype(F32)
                low = peak - high
                left = lax.broadcasted_iota(jnp.int32, (n_mp, 128), 1) < 64
                z32[pl.ds(c * 8 + counts[q], n_mp, stride=cap * 8), :] = jnp.where(left, high, low)
        y_out[q] = z32[...].astype(BF16).reshape(n_mp, cap * 8, 128)
        z_send(q, y_out, y_in, y_s, y_r)

    def ag1(q, h, k, f, p):
        at = ag[q].at[h, second[h], f]
        return remote(at, at, ag1_s.at[q, h, k], ag1_r.at[q, h, k], dp=dp_at(h, p, second[h]))

    def ag2(q, h, k, s, p):
        at = ag[q].at[h, s]
        return remote(at, at, ag2_s.at[q, h, k], ag2_r.at[q, h, k], dp=dp_at(h, first[h], p))

    sent = (counts[0] + 1, counts[1])
    for q in (many, few):
        z_wait(q, y_out, y_in, y_s, y_r)
        z32[...] = y_in[q].reshape(z32.shape).astype(F32)
        for r in range(sent[q]):
            v = z32[pl.ds(r, slots, stride=8), :].astype(BF16)
            v = jnp.dot(onehot_t, v, preferred_element_type=F32)
            for h in range(2):
                ag[q][h, second[h], first[h], r] = v[h * half:(h + 1) * half, :].astype(BF16)
        for k in range(1, side):
            for h in range(2):
                ag1(q, h, k, first[h], ahead(first[h], k, side)).start()
        for h in range(2):
            for k in range(1, side):
                f = behind(first[h], k, side)
                ag1(q, h, k, f, f).wait_recv()
            for k in range(1, side):
                ag2(q, h, k, second[h], ahead(second[h], k, side)).start()

    def spread(q, h, s):
        @pl.loop(0, side)
        def _(f):
            base = h * half * shard + dp_at(h, f, s) * rows + starts[q]
            for r in range(counts[q]):
                wide[pl.ds(base + r, half, stride=shard), :] = ag[q][h, s, f, r].astype(F32)

    for q in (many, few):
        for h in range(2):
            spread(q, h, second[h])
    for q in (many, few):
        for k in range(1, side):
            for h in range(2):
                s = behind(second[h], k, side)
                ag2(q, h, k, s, s).wait_recv()
                spread(q, h, s)

    both = []
    for h in range(2):
        peak = jnp.zeros((half, 128), F32)
        for s in range(side):
            for f in range(side):
                v = ag[few][h, s, f, counts[few]].astype(F32)
                peak = jnp.maximum(peak, v + pltpu.roll(v, 64, 1))
        both.append(peak)
    peak = jnp.concatenate(both, axis=0) + 1e-06
    z32[0:blocks, :] = 1.0 / peak
    scale_ref[...] = peak

    @pl.loop(0, blocks)
    def _(b):
        at = pl.ds(pl.multiple_of(b * shard, 16), shard)
        out_ref[at, :] = (wide[at, :] * z32[pl.ds(b, 1), :]).astype(BF16)

    for q in range(2):
        for h in range(2):
            for k in range(1, side):
                f, s = ahead(first[h], k, side), ahead(second[h], k, side)
                rs1(q, h, k, f).wait_send()
                rs2(q, h, k, s).wait_send()
                ag1(q, h, k, first[h], f).wait_send()
                ag2(q, h, k, second[h], s).wait_send()

    @pl.loop(1, n_dp)
    def _(k):
        to = ahead(dp, k, n_dp)
        remote(gram_out.at[to], gram_in.at[dp], g_s.at[k], g_r.at[k], dp=to).wait_send()
        remote(gram_all.at[dp], gram_all.at[dp], h_s.at[k], h_r.at[k], dp=to).wait_send()

    @pl.loop(0, n_mp - 1)
    def _(j):
        for q in range(2):
            z_copy(j, q, z_out, z_in, z_s, z_r).wait_send()
            z_copy(j, q, y_out, y_in, y_s, y_r).wait_send()


def body(gradients, owners, momentum, master):
    n_dp, n_mp = lax.axis_size("dp"), lax.axis_size("mp")
    _, blocks, shard, head = gradients.shape
    cap, _, rows, _ = momentum.shape
    slots = n_mp * cap
    moved = (cap, rows, n_mp, head)
    few, many, half = rows - 8, 8, blocks // 2
    sem = pltpu.SemaphoreType.DMA
    vmem = pl.BlockSpec(memory_space=pltpu.VMEM)
    out, scale, newmom, newmaster = pl.pallas_call(
        functools.partial(kernel, n_dp, n_mp, cap, blocks, rows),
        out_shape=(
            jax.ShapeDtypeStruct((blocks * shard, head), BF16),
            jax.ShapeDtypeStruct((blocks, head), F32),
            jax.ShapeDtypeStruct(moved, BF16),
            jax.ShapeDtypeStruct(moved, F32),
        ),
        in_specs=[pl.BlockSpec(memory_space=pl.ANY)] * 4,
        out_specs=(vmem,) * 4,
        scratch_shapes=[
            pltpu.SMEM((blocks,), jnp.int32),
            pltpu.VMEM((blocks * shard, head), BF16),
            pltpu.VMEM(moved, BF16),
            pltpu.VMEM(moved, F32),
            pltpu.VMEM((blocks * shard, head), F32),
            *[pltpu.VMEM((2, SIDE, SIDE, n, half, head), BF16) for n in (few, many)],
            *[pltpu.VMEM((2, SIDE, SIDE, n, half, head), BF16) for n in (few, many)],
            *[pltpu.VMEM((2, SIDE, n, half, head), BF16) for n in (few, many)],
            *[pltpu.VMEM((2, SIDE, n, half, head), BF16) for n in (few, many)],
            pltpu.VMEM((slots * 8, head), F32),
            pltpu.VMEM((2, n_mp, cap * 8, head), BF16),
            pltpu.VMEM((2, n_mp, cap * 8, head), BF16),
            pltpu.VMEM((cap, rows * n_mp, head), F32),
            *[pltpu.VMEM((n_dp, cap, head // n_dp, head), F32)] * 3,
            pltpu.VMEM((2, n_mp, cap * 8, head), BF16),
            pltpu.VMEM((2, n_mp, cap * 8, head), BF16),
            *[pltpu.VMEM((2, SIDE, SIDE, n, half, head), BF16) for n in (few + 1, many)],
            sem((4,)),
            *[sem((2, 2, SIDE))] * 4,
            *[sem((2, n_mp))] * 2,
            *[sem((n_dp,))] * 4,
            *[sem((2, n_mp))] * 2,
            *[sem((2, 2, SIDE))] * 4,
        ],
        compiler_params=pltpu.CompilerParams(
            collective_id=0, has_side_effects=True, vmem_limit_bytes=48 * 2**20),
        name="muon_step",
    )(
        owners,
        gradients.reshape(blocks * shard, head),
        momentum.transpose(0, 2, 1, 3),
        master.transpose(0, 2, 1, 3),
    )
    return (
        out.reshape(blocks, shard, head),
        scale[:, 0],
        newmom.transpose(0, 2, 1, 3),
        newmaster.transpose(0, 2, 1, 3),
    )


def solution(mesh):
    in_specs = (
        P("dp", None, "mp", None),
        P(),
        P("mp", None, "dp", None),
        P("mp", None, "dp", None),
    )
    out_specs = (P(None, "mp", None), P(), P("mp", None, "dp", None), P("mp", None, "dp", None))
    return jax.shard_map(body, mesh=mesh, in_specs=in_specs, out_specs=out_specs, check_vma=False)
```

```python
import functools
import math

import jax
import jax.numpy as jnp
from jax import lax
from jax.experimental import pallas as pl
from jax.experimental.pallas import tpu as pltpu
from jax.sharding import PartitionSpec as P

D = 7168
ITERS = 5
NEWTON = (3.4445, -4.775, 2.0315)
decay_rate = 0.95
learn_rate = 0.05
weight_decay = 0.1
update_gain = 0.2

MESH = pl.DeviceIdType.MESH
F32 = jnp.float32
BF16 = jnp.bfloat16
VMEM = 63 * 2**20
SIDE = 4


def dot(a, b):
    return jnp.dot(a, b, precision=lax.Precision.HIGHEST, preferred_element_type=F32)


def kernel(n_dp, n_mp, cap, blocks, rows, owners_hbm, grad_hbm, mom_hbm, master_hbm,
           out_hbm, scale_ref, newmom_hbm, newmaster_hbm,
           owners_ref, grad_ref, mom_ref, master_ref, wide, newmom_ref, newmaster_ref,
           rs1_out_a, rs1_out_b, rs1_in_a, rs1_in_b, rs2_out_a, rs2_out_b, rs2_in_a, rs2_in_b,
           z32, z_out, z_in, upd, gram_out, gram_in, gram_all, y_out, y_in, ag_a, ag_b,
           in_sem, out_sem, rs1_s, rs1_r, rs2_s, rs2_r, z_s, z_r, g_s, g_r, h_s, h_r, y_s, y_r,
           ag1_s, ag1_r, ag2_s, ag2_r):
    dp, mp = lax.axis_index("dp"), lax.axis_index("mp")
    side = SIDE
    x, y = dp // side, lax.rem(dp, side)
    slots = n_mp * cap
    shard = n_dp * rows
    half = blocks // 2
    few, many = 0, 1
    starts, counts = (8, 0), (rows - 8, 8)
    rs1_out, rs1_in = (rs1_out_a, rs1_out_b), (rs1_in_a, rs1_in_b)
    rs2_out, rs2_in = (rs2_out_a, rs2_out_b), (rs2_in_a, rs2_in_b)
    ag = (ag_a, ag_b)
    first, second = (x, y), (y, x)

    def dp_at(h, f, s):
        return f * side + s if h == 0 else s * side + f

    def ahead(v, k, n):
        return lax.rem(v + k, n)

    def behind(v, k, n):
        return lax.rem(v + n - k, n)

    def remote(src, dst, send, recv, **to):
        return pltpu.make_async_remote_copy(
            src_ref=src, dst_ref=dst, send_sem=send, recv_sem=recv, device_id=to, device_id_type=MESH)

    def all_sent(ref, sem):
        remote(ref, ref, sem, sem, dp=ahead(dp, 1, n_dp)).wait_send()

    def all_here(ref, sem):
        remote(ref, ref, sem, sem, dp=ahead(dp, 1, n_dp)).wait_recv()

    def z_offset(j):
        return n_mp // 2 + ((j + 1) // 2) * (1 - 2 * lax.rem(j, 2))

    loads = [
        pltpu.make_async_copy(src, dst, in_sem.at[i])
        for i, (src, dst) in enumerate((
            (grad_hbm.at[0:half * shard], grad_ref.at[0:half * shard]),
            (grad_hbm.at[half * shard:], grad_ref.at[half * shard:]),
            (owners_hbm, owners_ref), (mom_hbm, mom_ref), (master_hbm, master_ref)))
    ]
    for load in loads:
        load.start()

    barrier = pltpu.get_barrier_semaphore()

    @pl.loop(1, n_dp)
    def _(k):
        pl.semaphore_signal(barrier, 1, device_id={"dp": ahead(dp, k, n_dp)}, device_id_type=MESH)

    for h in range(2):
        loads[h].wait()

        @pl.loop(0, half)
        def _(i):
            if h == 0:
                pl.semaphore_signal(barrier, 1, device_id={"mp": ahead(mp, i + 1, n_mp)}, device_id_type=MESH)
            else:

                @pl.when(i > 0)
                def _():
                    pl.semaphore_signal(barrier, 1, device_id={"mp": behind(mp, i, n_mp)}, device_id_type=MESH)

            at = pl.ds(pl.multiple_of((h * half + i) * shard, 16), shard)
            wide[at, :] = grad_ref[at, :].astype(F32)

    def pick(q, h, f, dst):
        @pl.loop(0, side)
        def _(s):
            base = h * half * shard + dp_at(h, f, s) * rows + starts[q]
            for r in range(counts[q]):
                dst[s, r] = wide[pl.ds(base + r, half, stride=shard), :].astype(BF16)

    pl.semaphore_wait(barrier, n_dp + n_mp - 2)

    def rs1(q, h, f):
        return remote(rs1_out[q].at[h, f], rs1_in[q].at[h, first[h]], rs1_s.at[q, h], rs1_r.at[q, h],
                      dp=dp_at(h, f, second[h]))

    def rs2(q, h, s):
        return remote(rs2_out[q].at[h, s], rs2_in[q].at[h, second[h]], rs2_s.at[q, h], rs2_r.at[q, h],
                      dp=dp_at(h, first[h], s))

    for q in (few, many):
        for k in range(1, side):
            for h in range(2):
                f = ahead(first[h], k, side)
                pick(q, h, f, rs1_out[q].at[h, f])
                rs1(q, h, f).start()
        for h in range(2):
            pick(q, h, first[h], rs1_in[q].at[h, first[h]])

    loads[2].wait()
    lane = lax.broadcasted_iota(jnp.int32, (8, 128), 1)
    owner_row = jnp.full((8, 128), -1, jnp.int32)
    for b in range(blocks):
        owner_row = jnp.where(lane == b, owners_ref[b], owner_row)
    position = jnp.zeros((8, 128), jnp.int32)
    for b in range(blocks):
        position = position + jnp.where((owner_row == owners_ref[b]) & (lane > b), 1, 0)
    slot_row = jnp.where(owner_row >= 0, owner_row * cap + position, -1)[0:1, 0:blocks]
    place = jnp.broadcast_to(slot_row, (slots, blocks)) == lax.broadcasted_iota(jnp.int32, (slots, blocks), 0)
    onehot = jnp.where(place, 1.0, 0.0).astype(F32)
    onehot_t = onehot.T.astype(BF16)
    onehot = onehot.astype(BF16)
    count = jnp.int32(0)
    for b in range(blocks):
        count = count + jnp.where(owners_ref[b] == mp, 1, 0)

    z32[...] = jnp.zeros_like(z32)

    for q in (few, many):
        for h in range(2):
            all_here(rs1_in[q].at[h, 0:side - 1], rs1_r.at[q, h])
            for k in range(1, side + 1):
                s = ahead(second[h], k, side)
                for r in range(counts[q]):
                    total = rs1_in[q][h, 0, s, r].astype(F32)
                    for f in range(1, side):
                        total = total + rs1_in[q][h, f, s, r].astype(F32)
                    if k < side:
                        rs2_out[q][h, s, r] = total.astype(BF16)
                    else:
                        rs2_in[q][h, s, r] = total.astype(BF16)
                if k < side:
                    rs2(q, h, s).start()

    def z_copy(j, q, src, dst, s, r):
        to = ahead(mp, z_offset(j), n_mp)
        return remote(src.at[q, to], dst.at[q, mp], s.at[q], r.at[q], mp=to)

    def z_send(q, src, dst, s, r):
        @pl.loop(0, n_mp - 1)
        def _(j):
            z_copy(j, q, src, dst, s, r).start()

        dst[q, mp] = src[q, mp]

    for q in (few, many):
        for h in range(2):
            all_here(rs2_in[q].at[h, 0:side - 1], rs2_r.at[q, h])
        for r in range(counts[q]):
            both = []
            for h in range(2):
                total = rs2_in[q][h, 0, r].astype(F32)
                for s in range(1, side):
                    total = total + rs2_in[q][h, s, r].astype(F32)
                both.append(total)
            total = jnp.concatenate(both, axis=0).astype(BF16)
            z32[pl.ds(r, slots, stride=8), :] = jnp.dot(onehot, total, preferred_element_type=F32)
        z_out[q] = z32[...].astype(BF16).reshape(n_mp, cap * 8, 128)
        z_send(q, z_out, z_in, z_s, z_r)

    loads[3].wait()
    loads[4].wait()
    for q in (few, many):
        all_here(z_in.at[q, 0:n_mp - 1], z_r.at[q])
        z32[...] = z_in[q].reshape(z32.shape).astype(F32)
        for c in range(cap):
            for j in range(counts[q]):
                r = starts[q] + j
                arrived = z32[pl.ds(c * 8 + j, n_mp, stride=cap * 8), :]
                before = mom_ref[c, r]
                after = (decay_rate * before.astype(F32) + arrived).astype(BF16)
                newmom_ref[c, r] = jnp.where(count > c, after, before)
                upd[c, pl.ds(r * n_mp, n_mp), :] = arrived + decay_rate * after.astype(F32)

    stores = [pltpu.make_async_copy(newmom_ref, newmom_hbm, out_sem.at[0])]
    stores[0].start()

    piece = 128 // n_dp
    for c in range(cap):
        u = upd[c]
        gram = lax.dot_general(u, u, (((0,), (0,)), ((), ())), precision=lax.Precision.HIGHEST,
                               preferred_element_type=F32)
        for d in range(n_dp):
            gram_out[d, c] = gram[d * piece:(d + 1) * piece, :]

    @pl.loop(1, n_dp)
    def _(k):
        to = ahead(dp, k, n_dp)
        remote(gram_out.at[to], gram_in.at[dp], g_s, g_r, dp=to).start()

    gram_in[dp] = gram_out[dp]

    all_here(gram_in.at[0:n_dp - 1], g_r)

    part = gram_in[0]
    for s in range(1, n_dp):
        part = part + gram_in[s]
    gram_all[dp] = part

    @pl.loop(1, n_dp)
    def _(k):
        to = ahead(dp, k, n_dp)
        remote(gram_all.at[dp], gram_all.at[dp], h_s, h_r, dp=to).start()

    all_here(gram_all.at[0:n_dp - 1], h_r)

    eye = lax.broadcasted_iota(jnp.int32, (128, 128), 0) == lax.broadcasted_iota(jnp.int32, (128, 128), 1)
    a0, a1, a2 = NEWTON
    grams, norms = [], []
    for c in range(cap):
        raw = gram_all[:, c].reshape(128, 128)
        norm = jnp.sqrt(jnp.sum(jnp.where(eye, raw, 0.0), axis=(0, 1), keepdims=True)) + 1e-07
        grams.append(raw / (norm * norm))
        norms.append(norm)
    polys = [None] * cap
    for i in range(ITERS):
        mixes = [a1 * g + a2 * dot(g, g) for g in grams]
        if i == 0:
            polys = [jnp.where(eye, a0, 0.0) + m for m in mixes]
        else:
            polys = [a0 * p + dot(p, m) for p, m in zip(polys, mixes)]
        if i < ITERS - 1:
            halves = [a0 * g + dot(m, g) for g, m in zip(grams, mixes)]
            grams = [a0 * h + dot(h, m) for h, m in zip(halves, mixes)]
    polys = [p * (-learn_rate * update_gain * math.sqrt(D) / n) for p, n in zip(polys, norms)]

    peaks = [jnp.zeros((n_mp, 128), F32)] * cap
    for q in (many, few):
        for c in range(cap):
            at, size = starts[q] * n_mp, counts[q] * n_mp
            step = dot(upd[c, at:at + size, :], polys[c])
            for j in range(counts[q]):
                r = starts[q] + j
                before = master_ref[c, r]
                after = before * (1.0 - learn_rate * weight_decay) + step[j * n_mp:(j + 1) * n_mp, :]
                newmaster_ref[c, r] = jnp.where(count > c, after, before)
                peaks[c] = jnp.maximum(peaks[c], jnp.abs(after))
                z32[pl.ds(c * 8 + j, n_mp, stride=cap * 8), :] = after
            if q == few:
                peak = jnp.broadcast_to(jnp.max(peaks[c], axis=(0, 1), keepdims=True), (n_mp, 128))
                high = peak.astype(BF16).astype(F32)
                low = peak - high
                left = lax.broadcasted_iota(jnp.int32, (n_mp, 128), 1) < 64
                z32[pl.ds(c * 8 + counts[q], n_mp, stride=cap * 8), :] = jnp.where(left, high, low)
        y_out[q] = z32[...].astype(BF16).reshape(n_mp, cap * 8, 128)
        z_send(q, y_out, y_in, y_s, y_r)

    stores.append(pltpu.make_async_copy(newmaster_ref, newmaster_hbm, out_sem.at[1]))
    stores[1].start()

    def ag1(q, h, k, p):
        return remote(ag[q].at[h, second[h], 0], ag[q].at[h, second[h], k], ag1_s.at[q, h], ag1_r.at[q, h],
                      dp=dp_at(h, p, second[h]))

    def ag2(q, h, s, p, part):
        at = ag[q].at[h, s, 0] if part == 0 else ag[q].at[h, s, pl.ds(1, side - 1)]
        return remote(at, at, ag2_s.at[q, h, part], ag2_r.at[q, h, part], dp=dp_at(h, first[h], p))

    sent = (counts[0] + 1, counts[1])
    for q in (many, few):
        all_here(y_in.at[q, 0:n_mp - 1], y_r.at[q])
        z32[...] = y_in[q].reshape(z32.shape).astype(F32)
        for r in range(sent[q]):
            v = z32[pl.ds(r, slots, stride=8), :].astype(BF16)
            v = jnp.dot(onehot_t, v, preferred_element_type=F32)
            for h in range(2):
                ag[q][h, second[h], 0, r] = v[h * half:(h + 1) * half, :].astype(BF16)
        for k in range(1, side):
            for h in range(2):
                ag1(q, h, k, ahead(first[h], k, side)).start()
        for k in range(1, side):
            for h in range(2):
                ag2(q, h, second[h], ahead(second[h], k, side), 0).start()
        for h in range(2):
            all_here(ag[q].at[h, second[h], 1:side], ag1_r.at[q, h])
            for k in range(1, side):
                ag2(q, h, second[h], ahead(second[h], k, side), 1).start()

    def spread(q, h, s, k):
        f = behind(first[h], k, side)
        base = h * half * shard + dp_at(h, f, s) * rows + starts[q]
        for r in range(counts[q]):
            wide[pl.ds(base + r, half, stride=shard), :] = ag[q][h, s, k, r].astype(F32)

    for q in (many, few):
        for h in range(2):
            for k in range(side):
                spread(q, h, second[h], k)
    for q in (many, few):
        for part in range(2):
            for h in range(2):
                all_here(ag[q].at[h, 0:side - 1, 0] if part == 0 else ag[q].at[h, 0:side - 1, 1:side], ag2_r.at[q, h, part])
                for k in range(1, side):
                    s = behind(second[h], k, side)
                    if part == 0:
                        spread(q, h, s, 0)
                    else:
                        pl.loop(1, side)(functools.partial(spread, q, h, s))

    both = []
    for h in range(2):
        peak = jnp.zeros((half, 128), F32)
        for s in range(side):
            for f in range(side):
                v = ag[few][h, s, f, counts[few]].astype(F32)
                peak = jnp.maximum(peak, v + pltpu.roll(v, 64, 1))
        both.append(peak)
    peak = jnp.concatenate(both, axis=0) + 1e-06
    scale_ref[...] = peak.T[0:1, :]
    z32[0:blocks, :] = 1.0 / peak
    parts = 4
    step = blocks // parts
    for i in range(parts):

        @pl.loop(i * step, i * step + step)
        def _(b):
            at = pl.ds(pl.multiple_of(b * shard, 16), shard)
            grad_ref[at, :] = (wide[at, :] * z32[pl.ds(b, 1), :]).astype(BF16)

        part = pl.ds(i * step * shard, step * shard)
        stores.append(pltpu.make_async_copy(grad_ref.at[part], out_hbm.at[part], out_sem.at[2 + i]))
        stores[-1].start()
    for store in stores:
        store.wait()

    for q in range(2):
        all_sent(z_out.at[q, 0:n_mp - 1], z_s.at[q])
        all_sent(y_out.at[q, 0:n_mp - 1], y_s.at[q])
        for h in range(2):
            all_sent(rs1_out[q].at[h, 0:side - 1], rs1_s.at[q, h])
            all_sent(rs2_out[q].at[h, 0:side - 1], rs2_s.at[q, h])
            all_sent(ag[q].at[h, 0, 1:side], ag1_s.at[q, h])
            all_sent(ag[q].at[h, 0:side - 1, 0], ag2_s.at[q, h, 0])
            all_sent(ag[q].at[h, 0:side - 1, 1:side], ag2_s.at[q, h, 1])
    all_sent(gram_out.at[0:n_dp - 1], g_s)
    all_sent(gram_all.at[0:n_dp - 1], h_s)


def finish(out_in, scale_in, newmom_in, newmaster_in, out_hbm, scale_hbm, newmom_hbm, newmaster_hbm,
           out_ref, scale_ref, newmom_ref, newmaster_ref, in_sem, out_sem):
    parts = 4
    step = out_ref.shape[0] // parts
    ways = [(scale_in, scale_ref, scale_hbm)]
    for i in range(parts):
        at = pl.ds(i * step, step)
        ways.append((out_in.at[at], out_ref.at[at], out_hbm.at[at]))
    ways += [(newmaster_in, newmaster_ref, newmaster_hbm), (newmom_in, newmom_ref, newmom_hbm)]
    loads = [pltpu.make_async_copy(a, b, in_sem.at[i]) for i, (a, b, _) in enumerate(ways)]
    stores = [pltpu.make_async_copy(b, c, out_sem.at[i]) for i, (_, b, c) in enumerate(ways)]
    for load in loads:
        load.start()
    for load, store in zip(loads, stores):
        load.wait()
        store.start()
    for store in stores:
        store.wait()


def body(gradients, owners, momentum, master):
    n_dp, n_mp = lax.axis_size("dp"), lax.axis_size("mp")
    _, blocks, shard, head = gradients.shape
    cap, _, rows, _ = momentum.shape
    slots = n_mp * cap
    moved = (cap, rows, n_mp, head)
    few, many, half = rows - 8, 8, blocks // 2
    sem = pltpu.SemaphoreType.DMA
    hbm = pl.BlockSpec(memory_space=pltpu.HBM)
    vmem = pl.BlockSpec(memory_space=pltpu.VMEM)
    results = pl.pallas_call(
        functools.partial(kernel, n_dp, n_mp, cap, blocks, rows),
        out_shape=(
            jax.ShapeDtypeStruct((blocks * shard, head), BF16),
            jax.ShapeDtypeStruct((1, blocks), F32),
            jax.ShapeDtypeStruct(moved, BF16),
            jax.ShapeDtypeStruct(moved, F32),
        ),
        in_specs=[hbm] * 4,
        out_specs=(hbm, vmem, hbm, hbm),
        scratch_shapes=[
            pltpu.SMEM((blocks,), jnp.int32),
            pltpu.VMEM((blocks * shard, head), BF16),
            pltpu.VMEM(moved, BF16),
            pltpu.VMEM(moved, F32),
            pltpu.VMEM((blocks * shard, head), F32),
            pltpu.VMEM(moved, BF16),
            pltpu.VMEM(moved, F32),
            *[pltpu.VMEM((2, SIDE, SIDE, n, half, head), BF16) for n in (few, many)],
            *[pltpu.VMEM((2, SIDE, SIDE, n, half, head), BF16) for n in (few, many)],
            *[pltpu.VMEM((2, SIDE, n, half, head), BF16) for n in (few, many)],
            *[pltpu.VMEM((2, SIDE, n, half, head), BF16) for n in (few, many)],
            pltpu.VMEM((slots * 8, head), F32),
            pltpu.VMEM((2, n_mp, cap * 8, head), BF16),
            pltpu.VMEM((2, n_mp, cap * 8, head), BF16),
            pltpu.VMEM((cap, rows * n_mp, head), F32),
            *[pltpu.VMEM((n_dp, cap, head // n_dp, head), F32)] * 3,
            pltpu.VMEM((2, n_mp, cap * 8, head), BF16),
            pltpu.VMEM((2, n_mp, cap * 8, head), BF16),
            *[pltpu.VMEM((2, SIDE, SIDE, n, half, head), BF16) for n in (few + 1, many)],
            sem((5,)),
            sem((6,)),
            *[sem((2, 2))] * 4,
            *[sem((2,))] * 2,
            *[sem(())] * 4,
            *[sem((2,))] * 2,
            *[sem((2, 2))] * 2,
            *[sem((2, 2, 2))] * 2,
        ],
        compiler_params=pltpu.CompilerParams(
            collective_id=0, has_side_effects=True, vmem_limit_bytes=VMEM),
        name="muon_step",
    )(
        owners,
        gradients.reshape(blocks * shard, head),
        momentum.transpose(0, 2, 1, 3),
        master.transpose(0, 2, 1, 3),
    )
    out, scale, newmom, newmaster = pl.pallas_call(
        finish,
        out_shape=(
            jax.ShapeDtypeStruct((blocks * shard, head), BF16),
            jax.ShapeDtypeStruct((1, blocks), F32),
            jax.ShapeDtypeStruct(moved, BF16),
            jax.ShapeDtypeStruct(moved, F32),
        ),
        in_specs=[hbm] * 4,
        out_specs=[hbm] * 4,
        scratch_shapes=[
            pltpu.VMEM((blocks * shard, head), BF16),
            pltpu.VMEM((1, blocks), F32),
            pltpu.VMEM(moved, BF16),
            pltpu.VMEM(moved, F32),
            sem((7,)),
            sem((7,)),
        ],
        compiler_params=pltpu.CompilerParams(vmem_limit_bytes=VMEM),
        name="write_results",
    )(*results)
    return (
        out.reshape(blocks, shard, head),
        scale.reshape(blocks),
        newmom.transpose(0, 2, 1, 3),
        newmaster.transpose(0, 2, 1, 3),
    )


def solution(mesh):
    in_specs = (
        P("dp", None, "mp", None),
        P(),
        P("mp", None, "dp", None),
        P("mp", None, "dp", None),
    )
    out_specs = (P(None, "mp", None), P(), P("mp", None, "dp", None), P("mp", None, "dp", None))
    return jax.shard_map(body, mesh=mesh, in_specs=in_specs, out_specs=out_specs, check_vma=False)
```

```python
import functools
import math

import jax
import jax.numpy as jnp
from jax import lax
from jax.experimental import pallas as pl
from jax.experimental.pallas import tpu as pltpu
from jax.sharding import PartitionSpec as P

D = 7168
ITERS = 5
NEWTON = (3.4445, -4.775, 2.0315)
decay_rate = 0.95
learn_rate = 0.05
weight_decay = 0.1
update_gain = 0.2

MESH = pl.DeviceIdType.MESH
F32 = jnp.float32
BF16 = jnp.bfloat16
VMEM = 63 * 2**20
NEAR = (1, 2, 8, 13, 19, 24, 30, 31)
SIDE = 4


def dot(a, b):
    return jnp.dot(a, b, precision=lax.Precision.HIGHEST, preferred_element_type=F32)


def kernel(n_dp, n_mp, cap, blocks, rows, owners_hbm, grad_hbm, mom_hbm, master_hbm,
           out_hbm, scale_ref, newmom_hbm, newmaster_hbm,
           owners_ref, grad_ref, mom_ref, master_ref, wide, newmom_ref, newmaster_ref,
           rs1_out_a, rs1_out_b, rs1_in_a, rs1_in_b, rs2_out_a, rs2_out_b, rs2_in_a, rs2_in_b,
           z32, z_out, z_in, upd, gram_out, gram_in, gram_all, y_out, y_in, ag_a, ag_b,
           near_sem, in_sem, out_sem, rs1_s, rs1_r, rs2_s, rs2_r, z_s, z_r, g_s, g_r, h_s, h_r, y_s, y_r,
           ag1_s, ag1_r, ag2_s, ag2_r):
    dp, mp = lax.axis_index("dp"), lax.axis_index("mp")
    side = SIDE
    x, y = dp // side, lax.rem(dp, side)
    slots = n_mp * cap
    shard = n_dp * rows
    half = blocks // 2
    few, many = 0, 1
    starts, counts = (8, 0), (rows - 8, 8)
    rs1_out, rs1_in = (rs1_out_a, rs1_out_b), (rs1_in_a, rs1_in_b)
    rs2_out, rs2_in = (rs2_out_a, rs2_out_b), (rs2_in_a, rs2_in_b)
    ag = (ag_a, ag_b)
    first, second = (x, y), (y, x)

    def dp_at(h, f, s):
        return f * side + s if h == 0 else s * side + f

    def ahead(v, k, n):
        return lax.rem(v + k, n)

    def behind(v, k, n):
        return lax.rem(v + n - k, n)

    def remote(src, dst, send, recv, **to):
        return pltpu.make_async_remote_copy(
            src_ref=src, dst_ref=dst, send_sem=send, recv_sem=recv, device_id=to, device_id_type=MESH)

    def all_sent(ref, sem):
        remote(ref, ref, sem, sem, dp=ahead(dp, 1, n_dp)).wait_send()

    def all_here(ref, sem):
        remote(ref, ref, sem, sem, dp=ahead(dp, 1, n_dp)).wait_recv()

    def z_offset(j):
        return n_mp // 2 + ((j + 1) // 2) * (1 - 2 * lax.rem(j, 2))

    loads = [
        pltpu.make_async_copy(src, dst, in_sem.at[i])
        for i, (src, dst) in enumerate((
            (grad_hbm.at[0:half * shard], grad_ref.at[0:half * shard]),
            (grad_hbm.at[half * shard:], grad_ref.at[half * shard:]),
            (owners_hbm, owners_ref), (mom_hbm, mom_ref), (master_hbm, master_ref)))
    ]
    for load in loads:
        load.start()

    barrier = pltpu.get_barrier_semaphore()

    for k in range(1, side):
        for h in range(2):
            f = ahead(first[h], k, side)
            pl.semaphore_signal(barrier, 1, device_id={"dp": dp_at(h, f, second[h])}, device_id_type=MESH)
    for k in NEAR:
        pl.semaphore_signal(barrier, 1, device_id={"mp": ahead(mp, k, n_mp)}, device_id_type=MESH)

    for h in range(2):
        loads[h].wait()

        @pl.loop(0, half)
        def _(i):
            at = pl.ds(pl.multiple_of((h * half + i) * shard, 16), shard)
            wide[at, :] = grad_ref[at, :].astype(F32)

    def pick(q, h, f, dst):
        @pl.loop(0, side)
        def _(s):
            base = h * half * shard + dp_at(h, f, s) * rows + starts[q]
            for r in range(counts[q]):
                dst[s, r] = wide[pl.ds(base + r, half, stride=shard), :].astype(BF16)

    pl.semaphore_wait(barrier, 2 * (side - 1) + len(NEAR))

    def rs1(q, h, f):
        return remote(rs1_out[q].at[h, f], rs1_in[q].at[h, first[h]], rs1_s.at[q, h], rs1_r.at[q, h],
                      dp=dp_at(h, f, second[h]))

    def rs2(q, h, s):
        return remote(rs2_out[q].at[h, s], rs2_in[q].at[h, second[h]], rs2_s.at[q, h], rs2_r.at[q, h],
                      dp=dp_at(h, first[h], s))

    for q in (few, many):
        for k in range(1, side):
            for h in range(2):
                f = ahead(first[h], k, side)
                pick(q, h, f, rs1_out[q].at[h, f])
                rs1(q, h, f).start()
        for h in range(2):
            pick(q, h, first[h], rs1_in[q].at[h, first[h]])

    loads[2].wait()
    lane = lax.broadcasted_iota(jnp.int32, (8, 128), 1)
    owner_row = jnp.full((8, 128), -1, jnp.int32)
    for b in range(blocks):
        owner_row = jnp.where(lane == b, owners_ref[b], owner_row)
    position = jnp.zeros((8, 128), jnp.int32)
    for b in range(blocks):
        position = position + jnp.where((owner_row == owners_ref[b]) & (lane > b), 1, 0)
    slot_row = jnp.where(owner_row >= 0, owner_row * cap + position, -1)[0:1, 0:blocks]
    place = jnp.broadcast_to(slot_row, (slots, blocks)) == lax.broadcasted_iota(jnp.int32, (slots, blocks), 0)
    onehot = jnp.where(place, 1.0, 0.0).astype(F32)
    onehot_t = onehot.T.astype(BF16)
    onehot = onehot.astype(BF16)
    count = jnp.int32(0)
    for b in range(blocks):
        count = count + jnp.where(owners_ref[b] == mp, 1, 0)

    for k in NEAR:
        pl.semaphore_signal(near_sem, 1, device_id={"mp": ahead(mp, k, n_mp)}, device_id_type=MESH)
    z32[...] = jnp.zeros_like(z32)

    for q in (few, many):
        for h in range(2):
            all_here(rs1_in[q].at[h, 0:side - 1], rs1_r.at[q, h])
            for k in range(1, side + 1):
                s = ahead(second[h], k, side)
                for r in range(counts[q]):
                    total = rs1_in[q][h, 0, s, r].astype(F32)
                    for f in range(1, side):
                        total = total + rs1_in[q][h, f, s, r].astype(F32)
                    if k < side:
                        rs2_out[q][h, s, r] = total.astype(BF16)
                    else:
                        rs2_in[q][h, s, r] = total.astype(BF16)
                if k < side:
                    rs2(q, h, s).start()

    pl.semaphore_wait(near_sem, len(NEAR))

    def z_copy(j, q, src, dst, s, r):
        to = ahead(mp, z_offset(j), n_mp)
        return remote(src.at[q, to], dst.at[q, mp], s.at[q], r.at[q], mp=to)

    def z_send(q, src, dst, s, r):
        @pl.loop(0, n_mp - 1)
        def _(j):
            z_copy(j, q, src, dst, s, r).start()

        dst[q, mp] = src[q, mp]

    for q in (few, many):
        for h in range(2):
            all_here(rs2_in[q].at[h, 0:side - 1], rs2_r.at[q, h])
        for r in range(counts[q]):
            both = []
            for h in range(2):
                total = rs2_in[q][h, 0, r].astype(F32)
                for s in range(1, side):
                    total = total + rs2_in[q][h, s, r].astype(F32)
                both.append(total)
            total = jnp.concatenate(both, axis=0).astype(BF16)
            z32[pl.ds(r, slots, stride=8), :] = jnp.dot(onehot, total, preferred_element_type=F32)
        z_out[q] = z32[...].astype(BF16).reshape(n_mp, cap * 8, 128)
        z_send(q, z_out, z_in, z_s, z_r)

    loads[3].wait()
    loads[4].wait()
    for q in (few, many):
        all_here(z_in.at[q, 0:n_mp - 1], z_r.at[q])
        z32[...] = z_in[q].reshape(z32.shape).astype(F32)
        for c in range(cap):
            for j in range(counts[q]):
                r = starts[q] + j
                arrived = z32[pl.ds(c * 8 + j, n_mp, stride=cap * 8), :]
                before = mom_ref[c, r]
                after = (decay_rate * before.astype(F32) + arrived).astype(BF16)
                newmom_ref[c, r] = jnp.where(count > c, after, before)
                upd[c, pl.ds(r * n_mp, n_mp), :] = arrived + decay_rate * after.astype(F32)

    stores = [pltpu.make_async_copy(newmom_ref, newmom_hbm, out_sem.at[0])]
    stores[0].start()

    piece = 128 // n_dp
    for c in range(cap):
        u = upd[c]
        gram = lax.dot_general(u, u, (((0,), (0,)), ((), ())), precision=lax.Precision.HIGHEST,
                               preferred_element_type=F32)
        for d in range(n_dp):
            gram_out[d, c] = gram[d * piece:(d + 1) * piece, :]

    @pl.loop(1, n_dp)
    def _(k):
        to = ahead(dp, k, n_dp)
        remote(gram_out.at[to], gram_in.at[dp], g_s, g_r, dp=to).start()

    gram_in[dp] = gram_out[dp]

    all_here(gram_in.at[0:n_dp - 1], g_r)

    part = gram_in[0]
    for s in range(1, n_dp):
        part = part + gram_in[s]
    gram_all[dp] = part

    @pl.loop(1, n_dp)
    def _(k):
        to = ahead(dp, k, n_dp)
        remote(gram_all.at[dp], gram_all.at[dp], h_s, h_r, dp=to).start()

    all_here(gram_all.at[0:n_dp - 1], h_r)

    eye = lax.broadcasted_iota(jnp.int32, (128, 128), 0) == lax.broadcasted_iota(jnp.int32, (128, 128), 1)
    a0, a1, a2 = NEWTON
    grams, norms = [], []
    for c in range(cap):
        raw = gram_all[:, c].reshape(128, 128)
        norm = jnp.sqrt(jnp.sum(jnp.where(eye, raw, 0.0), axis=(0, 1), keepdims=True)) + 1e-07
        grams.append(raw / (norm * norm))
        norms.append(norm)
    polys = [None] * cap
    for i in range(ITERS):
        mixes = [a1 * g + a2 * dot(g, g) for g in grams]
        if i == 0:
            polys = [jnp.where(eye, a0, 0.0) + m for m in mixes]
        else:
            both = [dot(jnp.concatenate([p, g], axis=0), m) for p, g, m in zip(polys, grams, mixes)]
            polys = [a0 * p + b[0:128] for p, b in zip(polys, both)]
        if i < ITERS - 1:
            products = [b[128:] for b in both] if i else [dot(g, m) for g, m in zip(grams, mixes)]
            halves = [a0 * g + b for g, b in zip(grams, products)]
            grams = [a0 * h + dot(h, m) for h, m in zip(halves, mixes)]
    polys = [p * (-learn_rate * update_gain * math.sqrt(D) / n) for p, n in zip(polys, norms)]

    peaks = [jnp.zeros((n_mp, 128), F32)] * cap
    for q in (many, few):
        for c in range(cap):
            at, size = starts[q] * n_mp, counts[q] * n_mp
            step = dot(upd[c, at:at + size, :], polys[c])
            for j in range(counts[q]):
                r = starts[q] + j
                before = master_ref[c, r]
                after = before * (1.0 - learn_rate * weight_decay) + step[j * n_mp:(j + 1) * n_mp, :]
                newmaster_ref[c, r] = jnp.where(count > c, after, before)
                peaks[c] = jnp.maximum(peaks[c], jnp.abs(after))
                z32[pl.ds(c * 8 + j, n_mp, stride=cap * 8), :] = after
            if q == few:
                peak = jnp.broadcast_to(jnp.max(peaks[c], axis=(0, 1), keepdims=True), (n_mp, 128))
                high = peak.astype(BF16).astype(F32)
                low = peak - high
                left = lax.broadcasted_iota(jnp.int32, (n_mp, 128), 1) < 64
                z32[pl.ds(c * 8 + counts[q], n_mp, stride=cap * 8), :] = jnp.where(left, high, low)
        y_out[q] = z32[...].astype(BF16).reshape(n_mp, cap * 8, 128)
        z_send(q, y_out, y_in, y_s, y_r)

    stores.append(pltpu.make_async_copy(newmaster_ref, newmaster_hbm, out_sem.at[1]))
    stores[1].start()

    def ag1(q, h, k, p):
        return remote(ag[q].at[h, second[h], 0], ag[q].at[h, second[h], k], ag1_s.at[q, h], ag1_r.at[q, h],
                      dp=dp_at(h, p, second[h]))

    def ag2(q, h, s, p, part):
        at = ag[q].at[h, s, 0] if part == 0 else ag[q].at[h, s, pl.ds(1, side - 1)]
        return remote(at, at, ag2_s.at[q, h, part], ag2_r.at[q, h, part], dp=dp_at(h, first[h], p))

    sent = (counts[0] + 1, counts[1])
    for q in (many, few):
        all_here(y_in.at[q, 0:n_mp - 1], y_r.at[q])
        z32[...] = y_in[q].reshape(z32.shape).astype(F32)
        for r in range(sent[q]):
            v = z32[pl.ds(r, slots, stride=8), :].astype(BF16)
            v = jnp.dot(onehot_t, v, preferred_element_type=F32)
            for h in range(2):
                ag[q][h, second[h], 0, r] = v[h * half:(h + 1) * half, :].astype(BF16)
        for k in range(1, side):
            for h in range(2):
                ag1(q, h, k, ahead(first[h], k, side)).start()
        for k in range(1, side):
            for h in range(2):
                ag2(q, h, second[h], ahead(second[h], k, side), 0).start()
        for h in range(2):
            all_here(ag[q].at[h, second[h], 1:side], ag1_r.at[q, h])
            for k in range(1, side):
                ag2(q, h, second[h], ahead(second[h], k, side), 1).start()

    def spread(q, h, s, k):
        f = behind(first[h], k, side)
        base = h * half * shard + dp_at(h, f, s) * rows + starts[q]
        for r in range(counts[q]):
            wide[pl.ds(base + r, half, stride=shard), :] = ag[q][h, s, k, r].astype(F32)

    for q in (many, few):
        for h in range(2):
            for k in range(side):
                spread(q, h, second[h], k)
    for q in (many, few):
        for part in range(2):
            for h in range(2):
                all_here(ag[q].at[h, 0:side - 1, 0] if part == 0 else ag[q].at[h, 0:side - 1, 1:side], ag2_r.at[q, h, part])
                for k in range(1, side):
                    s = behind(second[h], k, side)
                    if part == 0:
                        spread(q, h, s, 0)
                    else:
                        pl.loop(1, side)(functools.partial(spread, q, h, s))

    both = []
    for h in range(2):
        peak = jnp.zeros((half, 128), F32)
        for s in range(side):
            for f in range(side):
                v = ag[few][h, s, f, counts[few]].astype(F32)
                peak = jnp.maximum(peak, v + pltpu.roll(v, 64, 1))
        both.append(peak)
    peak = jnp.concatenate(both, axis=0) + 1e-06
    scale_ref[...] = peak.T[0:1, :]
    z32[0:blocks, :] = 1.0 / peak
    parts = 4
    step = blocks // parts
    for i in range(parts):

        @pl.loop(i * step, i * step + step)
        def _(b):
            at = pl.ds(pl.multiple_of(b * shard, 16), shard)
            grad_ref[at, :] = (wide[at, :] * z32[pl.ds(b, 1), :]).astype(BF16)

        part = pl.ds(i * step * shard, step * shard)
        stores.append(pltpu.make_async_copy(grad_ref.at[part], out_hbm.at[part], out_sem.at[2 + i]))
        stores[-1].start()
    for store in stores:
        store.wait()

    for q in range(2):
        all_sent(z_out.at[q, 0:n_mp - 1], z_s.at[q])
        all_sent(y_out.at[q, 0:n_mp - 1], y_s.at[q])
        for h in range(2):
            all_sent(rs1_out[q].at[h, 0:side - 1], rs1_s.at[q, h])
            all_sent(rs2_out[q].at[h, 0:side - 1], rs2_s.at[q, h])
            all_sent(ag[q].at[h, 0, 1:side], ag1_s.at[q, h])
            all_sent(ag[q].at[h, 0:side - 1, 0], ag2_s.at[q, h, 0])
            all_sent(ag[q].at[h, 0:side - 1, 1:side], ag2_s.at[q, h, 1])
    all_sent(gram_out.at[0:n_dp - 1], g_s)
    all_sent(gram_all.at[0:n_dp - 1], h_s)


def finish(out_in, scale_in, newmom_in, newmaster_in, out_hbm, scale_hbm, newmom_hbm, newmaster_hbm,
           out_ref, scale_ref, newmom_ref, newmaster_ref, in_sem, out_sem):
    parts = 4
    step = out_ref.shape[0] // parts
    ways = [(scale_in, scale_ref, scale_hbm)]
    for i in range(parts):
        at = pl.ds(i * step, step)
        ways.append((out_in.at[at], out_ref.at[at], out_hbm.at[at]))
    ways += [(newmaster_in, newmaster_ref, newmaster_hbm), (newmom_in, newmom_ref, newmom_hbm)]
    loads = [pltpu.make_async_copy(a, b, in_sem.at[i]) for i, (a, b, _) in enumerate(ways)]
    stores = [pltpu.make_async_copy(b, c, out_sem.at[i]) for i, (_, b, c) in enumerate(ways)]
    for load in loads:
        load.start()
    for load, store in zip(loads, stores):
        load.wait()
        store.start()
    for store in stores:
        store.wait()


def body(gradients, owners, momentum, master):
    n_dp, n_mp = lax.axis_size("dp"), lax.axis_size("mp")
    _, blocks, shard, head = gradients.shape
    cap, _, rows, _ = momentum.shape
    slots = n_mp * cap
    moved = (cap, rows, n_mp, head)
    few, many, half = rows - 8, 8, blocks // 2
    sem = pltpu.SemaphoreType.DMA
    hbm = pl.BlockSpec(memory_space=pltpu.HBM)
    vmem = pl.BlockSpec(memory_space=pltpu.VMEM)
    results = pl.pallas_call(
        functools.partial(kernel, n_dp, n_mp, cap, blocks, rows),
        out_shape=(
            jax.ShapeDtypeStruct((blocks * shard, head), BF16),
            jax.ShapeDtypeStruct((1, blocks), F32),
            jax.ShapeDtypeStruct(moved, BF16),
            jax.ShapeDtypeStruct(moved, F32),
        ),
        in_specs=[hbm] * 4,
        out_specs=(hbm, vmem, hbm, hbm),
        scratch_shapes=[
            pltpu.SMEM((blocks,), jnp.int32),
            pltpu.VMEM((blocks * shard, head), BF16),
            pltpu.VMEM(moved, BF16),
            pltpu.VMEM(moved, F32),
            pltpu.VMEM((blocks * shard, head), F32),
            pltpu.VMEM(moved, BF16),
            pltpu.VMEM(moved, F32),
            *[pltpu.VMEM((2, SIDE, SIDE, n, half, head), BF16) for n in (few, many)],
            *[pltpu.VMEM((2, SIDE, SIDE, n, half, head), BF16) for n in (few, many)],
            *[pltpu.VMEM((2, SIDE, n, half, head), BF16) for n in (few, many)],
            *[pltpu.VMEM((2, SIDE, n, half, head), BF16) for n in (few, many)],
            pltpu.VMEM((slots * 8, head), F32),
            pltpu.VMEM((2, n_mp, cap * 8, head), BF16),
            pltpu.VMEM((2, n_mp, cap * 8, head), BF16),
            pltpu.VMEM((cap, rows * n_mp, head), F32),
            *[pltpu.VMEM((n_dp, cap, head // n_dp, head), F32)] * 3,
            pltpu.VMEM((2, n_mp, cap * 8, head), BF16),
            pltpu.VMEM((2, n_mp, cap * 8, head), BF16),
            *[pltpu.VMEM((2, SIDE, SIDE, n, half, head), BF16) for n in (few + 1, many)],
            pltpu.SemaphoreType.REGULAR,
            sem((5,)),
            sem((6,)),
            *[sem((2, 2))] * 4,
            *[sem((2,))] * 2,
            *[sem(())] * 4,
            *[sem((2,))] * 2,
            *[sem((2, 2))] * 2,
            *[sem((2, 2, 2))] * 2,
        ],
        compiler_params=pltpu.CompilerParams(
            collective_id=0, has_side_effects=True, vmem_limit_bytes=VMEM),
        name="muon_step",
    )(
        owners,
        gradients.reshape(blocks * shard, head),
        momentum.transpose(0, 2, 1, 3),
        master.transpose(0, 2, 1, 3),
    )
    out, scale, newmom, newmaster = pl.pallas_call(
        finish,
        out_shape=(
            jax.ShapeDtypeStruct((blocks * shard, head), BF16),
            jax.ShapeDtypeStruct((1, blocks), F32),
            jax.ShapeDtypeStruct(moved, BF16),
            jax.ShapeDtypeStruct(moved, F32),
        ),
        in_specs=[hbm] * 4,
        out_specs=[hbm] * 4,
        scratch_shapes=[
            pltpu.VMEM((blocks * shard, head), BF16),
            pltpu.VMEM((1, blocks), F32),
            pltpu.VMEM(moved, BF16),
            pltpu.VMEM(moved, F32),
            sem((7,)),
            sem((7,)),
        ],
        compiler_params=pltpu.CompilerParams(vmem_limit_bytes=VMEM),
        name="write_results",
    )(*results)
    return (
        out.reshape(blocks, shard, head),
        scale.reshape(blocks),
        newmom.transpose(0, 2, 1, 3),
        newmaster.transpose(0, 2, 1, 3),
    )


def solution(mesh):
    in_specs = (
        P("dp", None, "mp", None),
        P(),
        P("mp", None, "dp", None),
        P("mp", None, "dp", None),
    )
    out_specs = (P(None, "mp", None), P(), P("mp", None, "dp", None), P("mp", None, "dp", None))
    return jax.shard_map(body, mesh=mesh, in_specs=in_specs, out_specs=out_specs, check_vma=False)
```

```python
import functools
import math

import jax
import jax.numpy as jnp
from jax import lax
from jax.experimental import pallas as pl
from jax.experimental.pallas import tpu as pltpu
from jax.sharding import PartitionSpec as P

D = 7168
ITERS = 5
NEWTON = (3.4445, -4.775, 2.0315)
decay_rate = 0.95
learn_rate = 0.05
weight_decay = 0.1
update_gain = 0.2

MESH = pl.DeviceIdType.MESH
F32 = jnp.float32
BF16 = jnp.bfloat16
VMEM = 63 * 2**20
NEAR = (1, 2, 8, 13, 19, 24, 30, 31)
SIDE = 4


def dot(a, b):
    return jnp.dot(a, b, precision=lax.Precision.HIGHEST, preferred_element_type=F32)


def kernel(n_dp, n_mp, cap, blocks, rows, owners_hbm, grad_hbm, mom_hbm, master_hbm,
           out_hbm, scale_ref, newmom_hbm, newmaster_hbm,
           owners_ref, grad_ref, mom_ref, master_ref, wide, newmom_ref, newmaster_ref,
           rs1_out_a, rs1_out_b, rs1_in_a, rs1_in_b, rs2_out_a, rs2_out_b, rs2_in_a, rs2_in_b,
           z32, z_out, z_in, upd, gram_out, gram_in, gram_all, y_out, y_in, ag_a, ag_b,
           near_sem, in_sem, out_sem, rs1_s, rs1_r, rs2_s, rs2_r, z_s, z_r, g_s, g_r, h_s, h_r, y_s, y_r,
           ag1_s, ag1_r, ag2_s, ag2_r):
    dp, mp = lax.axis_index("dp"), lax.axis_index("mp")
    side = SIDE
    x, y = dp // side, lax.rem(dp, side)
    slots = n_mp * cap
    shard = n_dp * rows
    half = blocks // 2
    few, many = 0, 1
    starts, counts = (8, 0), (rows - 8, 8)
    rs1_out, rs1_in = (rs1_out_a, rs1_out_b), (rs1_in_a, rs1_in_b)
    rs2_out, rs2_in = (rs2_out_a, rs2_out_b), (rs2_in_a, rs2_in_b)
    ag = (ag_a, ag_b)
    first, second = (x, y), (y, x)

    def dp_at(h, f, s):
        return f * side + s if h == 0 else s * side + f

    def ahead(v, k, n):
        return lax.rem(v + k, n)

    def behind(v, k, n):
        return lax.rem(v + n - k, n)

    def remote(src, dst, send, recv, **to):
        return pltpu.make_async_remote_copy(
            src_ref=src, dst_ref=dst, send_sem=send, recv_sem=recv, device_id=to, device_id_type=MESH)

    def all_sent(ref, sem):
        remote(ref, ref, sem, sem, dp=ahead(dp, 1, n_dp)).wait_send()

    def all_here(ref, sem):
        remote(ref, ref, sem, sem, dp=ahead(dp, 1, n_dp)).wait_recv()

    def z_offset(j):
        return n_mp // 2 + ((j + 1) // 2) * (1 - 2 * lax.rem(j, 2))

    loads = [
        pltpu.make_async_copy(src, dst, in_sem.at[i])
        for i, (src, dst) in enumerate((
            (grad_hbm.at[0:half * shard], grad_ref.at[0:half * shard]),
            (grad_hbm.at[half * shard:], grad_ref.at[half * shard:]),
            (owners_hbm, owners_ref), (mom_hbm, mom_ref), (master_hbm, master_ref)))
    ]
    for load in loads:
        load.start()

    barrier = pltpu.get_barrier_semaphore()

    for k in range(1, side):
        for h in range(2):
            f = ahead(first[h], k, side)
            pl.semaphore_signal(barrier, 1, device_id={"dp": dp_at(h, f, second[h])}, device_id_type=MESH)
    for k in NEAR:
        pl.semaphore_signal(barrier, 1, device_id={"mp": ahead(mp, k, n_mp)}, device_id_type=MESH)

    for h in range(2):
        loads[h].wait()

        @pl.loop(0, half)
        def _(i):
            at = pl.ds(pl.multiple_of((h * half + i) * shard, 16), shard)
            wide[at, :] = grad_ref[at, :].astype(F32)

    def pick(q, h, f, dst):
        @pl.loop(0, side)
        def _(s):
            base = h * half * shard + dp_at(h, f, s) * rows + starts[q]
            for r in range(counts[q]):
                dst[s, r] = wide[pl.ds(base + r, half, stride=shard), :].astype(BF16)

    pl.semaphore_wait(barrier, 2 * (side - 1) + len(NEAR))

    def rs1(q, h, f):
        return remote(rs1_out[q].at[h, f], rs1_in[q].at[h, first[h]], rs1_s.at[q, h], rs1_r.at[q, h],
                      dp=dp_at(h, f, second[h]))

    def rs2(q, h, s):
        return remote(rs2_out[q].at[h, s], rs2_in[q].at[h, second[h]], rs2_s.at[q, h], rs2_r.at[q, h],
                      dp=dp_at(h, first[h], s))

    for q in (few, many):
        for k in range(1, side):
            for h in range(2):
                f = ahead(first[h], k, side)
                pick(q, h, f, rs1_out[q].at[h, f])
                rs1(q, h, f).start()
        for h in range(2):
            pick(q, h, first[h], rs1_in[q].at[h, first[h]])

    loads[2].wait()
    lane = lax.broadcasted_iota(jnp.int32, (8, 128), 1)
    owner_row = jnp.full((8, 128), -1, jnp.int32)
    for b in range(blocks):
        owner_row = jnp.where(lane == b, owners_ref[b], owner_row)
    position = jnp.zeros((8, 128), jnp.int32)
    for b in range(blocks):
        position = position + jnp.where((owner_row == owners_ref[b]) & (lane > b), 1, 0)
    slot_row = jnp.where(owner_row >= 0, owner_row * cap + position, -1)[0:1, 0:blocks]
    place = jnp.broadcast_to(slot_row, (slots, blocks)) == lax.broadcasted_iota(jnp.int32, (slots, blocks), 0)
    onehot = jnp.where(place, 1.0, 0.0).astype(F32)
    onehot_t = onehot.T.astype(BF16)
    onehot = onehot.astype(BF16)
    count = jnp.int32(0)
    for b in range(blocks):
        count = count + jnp.where(owners_ref[b] == mp, 1, 0)

    for k in NEAR:
        pl.semaphore_signal(near_sem, 1, device_id={"mp": ahead(mp, k, n_mp)}, device_id_type=MESH)
    z32[...] = jnp.zeros_like(z32)

    def z_copy(j, q, src, dst, s, r):
        to = ahead(mp, z_offset(j), n_mp)
        return remote(src.at[q, to], dst.at[q, mp], s.at[q], r.at[q], mp=to)

    def z_send(q, src, dst, s, r):
        @pl.loop(0, n_mp - 1)
        def _(j):
            z_copy(j, q, src, dst, s, r).start()

        dst[q, mp] = src[q, mp]

    for q in (few, many):
        for h in range(2):
            all_here(rs1_in[q].at[h, 0:side - 1], rs1_r.at[q, h])
            for k in range(1, side + 1):
                s = ahead(second[h], k, side)
                for r in range(counts[q]):
                    total = rs1_in[q][h, 0, s, r].astype(F32)
                    for f in range(1, side):
                        total = total + rs1_in[q][h, f, s, r].astype(F32)
                    if k < side:
                        rs2_out[q][h, s, r] = total.astype(BF16)
                    else:
                        rs2_in[q][h, s, r] = total.astype(BF16)
                if k < side:
                    rs2(q, h, s).start()
        if q == few:
            pl.semaphore_wait(near_sem, len(NEAR))
        for h in range(2):
            all_here(rs2_in[q].at[h, 0:side - 1], rs2_r.at[q, h])
        for r in range(counts[q]):
            both = []
            for h in range(2):
                total = rs2_in[q][h, 0, r].astype(F32)
                for s in range(1, side):
                    total = total + rs2_in[q][h, s, r].astype(F32)
                both.append(total)
            total = jnp.concatenate(both, axis=0).astype(BF16)
            z32[pl.ds(r, slots, stride=8), :] = jnp.dot(onehot, total, preferred_element_type=F32)
        z_out[q] = z32[...].astype(BF16).reshape(n_mp, cap * 8, 128)
        z_send(q, z_out, z_in, z_s, z_r)

    loads[3].wait()
    loads[4].wait()
    for q in (few, many):
        all_here(z_in.at[q, 0:n_mp - 1], z_r.at[q])
        z32[...] = z_in[q].reshape(z32.shape).astype(F32)
        for c in range(cap):
            for j in range(counts[q]):
                r = starts[q] + j
                arrived = z32[pl.ds(c * 8 + j, n_mp, stride=cap * 8), :]
                before = mom_ref[c, r]
                after = (decay_rate * before.astype(F32) + arrived).astype(BF16)
                newmom_ref[c, r] = jnp.where(count > c, after, before)
                upd[c, pl.ds(r * n_mp, n_mp), :] = arrived + decay_rate * after.astype(F32)

    stores = [pltpu.make_async_copy(newmom_ref, newmom_hbm, out_sem.at[0])]
    stores[0].start()

    piece = 128 // n_dp
    for c in range(cap):
        u = upd[c]
        gram = lax.dot_general(u, u, (((0,), (0,)), ((), ())), precision=lax.Precision.HIGHEST,
                               preferred_element_type=F32)
        for d in range(n_dp):
            gram_out[d, c] = gram[d * piece:(d + 1) * piece, :]

    for k in (10, 9, 11, 6, 14, 5, 7, 13, 15, 2, 8, 1, 3, 4, 12):
        to = ahead(dp, k, n_dp)
        remote(gram_out.at[to], gram_in.at[dp], g_s, g_r, dp=to).start()

    gram_in[dp] = gram_out[dp]

    all_here(gram_in.at[0:n_dp - 1], g_r)

    part = gram_in[0]
    for s in range(1, n_dp):
        part = part + gram_in[s]
    gram_all[dp] = part

    for k in (10, 9, 11, 6, 14, 5, 7, 13, 15, 2, 8, 1, 3, 4, 12):
        to = ahead(dp, k, n_dp)
        remote(gram_all.at[dp], gram_all.at[dp], h_s, h_r, dp=to).start()

    all_here(gram_all.at[0:n_dp - 1], h_r)

    eye = lax.broadcasted_iota(jnp.int32, (128, 128), 0) == lax.broadcasted_iota(jnp.int32, (128, 128), 1)
    a0, a1, a2 = NEWTON
    grams, norms = [], []
    for c in range(cap):
        raw = gram_all[:, c].reshape(128, 128)
        norm = jnp.sqrt(jnp.sum(jnp.where(eye, raw, 0.0), axis=(0, 1), keepdims=True)) + 1e-07
        grams.append(raw / (norm * norm))
        norms.append(norm)
    polys = [None] * cap
    for i in range(ITERS):
        mixes = [a1 * g + a2 * dot(g, g) for g in grams]
        if i == 0:
            polys = [jnp.where(eye, a0, 0.0) + m for m in mixes]
        else:
            both = [dot(jnp.concatenate([p, g], axis=0), m) for p, g, m in zip(polys, grams, mixes)]
            polys = [a0 * p + b[0:128] for p, b in zip(polys, both)]
        if i < ITERS - 1:
            products = [b[128:] for b in both] if i else [dot(g, m) for g, m in zip(grams, mixes)]
            halves = [a0 * g + b for g, b in zip(grams, products)]
            grams = [a0 * h + dot(h, m) for h, m in zip(halves, mixes)]
    polys = [p * (-learn_rate * update_gain * math.sqrt(D) / n) for p, n in zip(polys, norms)]

    peaks = [jnp.zeros((n_mp, 128), F32)] * cap
    for q in (many, few):
        for c in range(cap):
            at, size = starts[q] * n_mp, counts[q] * n_mp
            step = dot(upd[c, at:at + size, :], polys[c])
            for j in range(counts[q]):
                r = starts[q] + j
                before = master_ref[c, r]
                after = before * (1.0 - learn_rate * weight_decay) + step[j * n_mp:(j + 1) * n_mp, :]
                newmaster_ref[c, r] = jnp.where(count > c, after, before)
                peaks[c] = jnp.maximum(peaks[c], jnp.abs(after))
                z32[pl.ds(c * 8 + j, n_mp, stride=cap * 8), :] = after
            if q == few:
                peak = jnp.broadcast_to(jnp.max(peaks[c], axis=(0, 1), keepdims=True), (n_mp, 128))
                high = peak.astype(BF16).astype(F32)
                low = peak - high
                left = lax.broadcasted_iota(jnp.int32, (n_mp, 128), 1) < 64
                z32[pl.ds(c * 8 + counts[q], n_mp, stride=cap * 8), :] = jnp.where(left, high, low)
        y_out[q] = z32[...].astype(BF16).reshape(n_mp, cap * 8, 128)
        z_send(q, y_out, y_in, y_s, y_r)

    stores.append(pltpu.make_async_copy(newmaster_ref, newmaster_hbm, out_sem.at[1]))
    stores[1].start()

    def ag1(q, h, k, p):
        return remote(ag[q].at[h, second[h], 0], ag[q].at[h, second[h], k], ag1_s.at[q, h, k], ag1_r.at[q, h, k],
                      dp=dp_at(h, p, second[h]))

    def ag2(q, h, s, p, part):
        at = ag[q].at[h, s, part]
        return remote(at, at, ag2_s.at[q, h, part], ag2_r.at[q, h, part], dp=dp_at(h, first[h], p))

    sent = (counts[0] + 1, counts[1])
    for q in (many, few):
        all_here(y_in.at[q, 0:n_mp - 1], y_r.at[q])
        z32[...] = y_in[q].reshape(z32.shape).astype(F32)
        for r in range(sent[q]):
            v = z32[pl.ds(r, slots, stride=8), :].astype(BF16)
            v = jnp.dot(onehot_t, v, preferred_element_type=F32)
            for h in range(2):
                ag[q][h, second[h], 0, r] = v[h * half:(h + 1) * half, :].astype(BF16)
        for k in range(1, side):
            for h in range(2):
                ag1(q, h, k, ahead(first[h], k, side)).start()
        for k in range(1, side):
            for h in range(2):
                ag2(q, h, second[h], ahead(second[h], k, side), 0).start()
        for c in (1, 3, 2):
            for h in range(2):
                at = ag[q].at[h, second[h], c]
                remote(at, at, ag1_s.at[q, h, c], ag1_r.at[q, h, c], dp=ahead(dp, 1, n_dp)).wait_recv()
                for k in (2, 1, 3):
                    ag2(q, h, second[h], ahead(second[h], k, side), c).start()

    def spread(q, h, s, k):
        f = behind(first[h], k, side)
        base = h * half * shard + dp_at(h, f, s) * rows + starts[q]
        for r in range(counts[q]):
            wide[pl.ds(base + r, half, stride=shard), :] = ag[q][h, s, k, r].astype(F32)

    for q in (many, few):
        for h in range(2):
            for k in range(side):
                spread(q, h, second[h], k)
    for q in (many, few):
        for part in (0, 1, 3, 2):
            for h in range(2):
                all_here(ag[q].at[h, 0:side - 1, part], ag2_r.at[q, h, part])
                for k in range(1, side):
                    s = behind(second[h], k, side)
                    spread(q, h, s, part)

    both = []
    for h in range(2):
        peak = jnp.zeros((half, 128), F32)
        for s in range(side):
            for f in range(side):
                v = ag[few][h, s, f, counts[few]].astype(F32)
                peak = jnp.maximum(peak, v + pltpu.roll(v, 64, 1))
        both.append(peak)
    peak = jnp.concatenate(both, axis=0) + 1e-06
    scale_ref[...] = peak.T[0:1, :]
    z32[0:blocks, :] = 1.0 / peak
    parts = 4
    step = blocks // parts
    for i in range(parts):

        @pl.loop(i * step, i * step + step)
        def _(b):
            at = pl.ds(pl.multiple_of(b * shard, 16), shard)
            grad_ref[at, :] = (wide[at, :] * z32[pl.ds(b, 1), :]).astype(BF16)

        part = pl.ds(i * step * shard, step * shard)
        stores.append(pltpu.make_async_copy(grad_ref.at[part], out_hbm.at[part], out_sem.at[2 + i]))
        stores[-1].start()
    for store in stores:
        store.wait()

    for q in range(2):
        all_sent(z_out.at[q, 0:n_mp - 1], z_s.at[q])
        all_sent(y_out.at[q, 0:n_mp - 1], y_s.at[q])
        for h in range(2):
            all_sent(rs1_out[q].at[h, 0:side - 1], rs1_s.at[q, h])
            all_sent(rs2_out[q].at[h, 0:side - 1], rs2_s.at[q, h])
            for c in range(side):
                if c:
                    all_sent(ag[q].at[h, 0, c], ag1_s.at[q, h, c])
                all_sent(ag[q].at[h, 0:side - 1, c], ag2_s.at[q, h, c])
    all_sent(gram_out.at[0:n_dp - 1], g_s)
    all_sent(gram_all.at[0:n_dp - 1], h_s)


def finish(out_in, scale_in, newmom_in, newmaster_in, out_hbm, scale_hbm, newmom_hbm, newmaster_hbm,
           out_ref, scale_ref, newmom_ref, newmaster_ref, in_sem, out_sem):
    parts = 4
    step = out_ref.shape[0] // parts
    ways = [(scale_in, scale_ref, scale_hbm)]
    for i in range(parts):
        at = pl.ds(i * step, step)
        ways.append((out_in.at[at], out_ref.at[at], out_hbm.at[at]))
    ways += [(newmaster_in, newmaster_ref, newmaster_hbm), (newmom_in, newmom_ref, newmom_hbm)]
    loads = [pltpu.make_async_copy(a, b, in_sem.at[i]) for i, (a, b, _) in enumerate(ways)]
    stores = [pltpu.make_async_copy(b, c, out_sem.at[i]) for i, (_, b, c) in enumerate(ways)]
    for load in loads:
        load.start()
    for load, store in zip(loads, stores):
        load.wait()
        store.start()
    for store in stores:
        store.wait()


def body(gradients, owners, momentum, master):
    n_dp, n_mp = lax.axis_size("dp"), lax.axis_size("mp")
    _, blocks, shard, head = gradients.shape
    cap, _, rows, _ = momentum.shape
    slots = n_mp * cap
    moved = (cap, rows, n_mp, head)
    few, many, half = rows - 8, 8, blocks // 2
    sem = pltpu.SemaphoreType.DMA
    hbm = pl.BlockSpec(memory_space=pltpu.HBM)
    vmem = pl.BlockSpec(memory_space=pltpu.VMEM)
    results = pl.pallas_call(
        functools.partial(kernel, n_dp, n_mp, cap, blocks, rows),
        out_shape=(
            jax.ShapeDtypeStruct((blocks * shard, head), BF16),
            jax.ShapeDtypeStruct((1, blocks), F32),
            jax.ShapeDtypeStruct(moved, BF16),
            jax.ShapeDtypeStruct(moved, F32),
        ),
        in_specs=[hbm] * 4,
        out_specs=(hbm, vmem, hbm, hbm),
        scratch_shapes=[
            pltpu.SMEM((blocks,), jnp.int32),
            pltpu.VMEM((blocks * shard, head), BF16),
            pltpu.VMEM(moved, BF16),
            pltpu.VMEM(moved, F32),
            pltpu.VMEM((blocks * shard, head), F32),
            pltpu.VMEM(moved, BF16),
            pltpu.VMEM(moved, F32),
            *[pltpu.VMEM((2, SIDE, SIDE, n, half, head), BF16) for n in (few, many)],
            *[pltpu.VMEM((2, SIDE, SIDE, n, half, head), BF16) for n in (few, many)],
            *[pltpu.VMEM((2, SIDE, n, half, head), BF16) for n in (few, many)],
            *[pltpu.VMEM((2, SIDE, n, half, head), BF16) for n in (few, many)],
            pltpu.VMEM((slots * 8, head), F32),
            pltpu.VMEM((2, n_mp, cap * 8, head), BF16),
            pltpu.VMEM((2, n_mp, cap * 8, head), BF16),
            pltpu.VMEM((cap, rows * n_mp, head), F32),
            *[pltpu.VMEM((n_dp, cap, head // n_dp, head), F32)] * 3,
            pltpu.VMEM((2, n_mp, cap * 8, head), BF16),
            pltpu.VMEM((2, n_mp, cap * 8, head), BF16),
            *[pltpu.VMEM((2, SIDE, SIDE, n, half, head), BF16) for n in (few + 1, many)],
            pltpu.SemaphoreType.REGULAR,
            sem((5,)),
            sem((6,)),
            *[sem((2, 2))] * 4,
            *[sem((2,))] * 2,
            *[sem(())] * 4,
            *[sem((2,))] * 2,
            *[sem((2, 2, SIDE))] * 4,
        ],
        compiler_params=pltpu.CompilerParams(
            collective_id=0, has_side_effects=True, vmem_limit_bytes=VMEM),
        name="muon_step",
    )(
        owners,
        gradients.reshape(blocks * shard, head),
        momentum.transpose(0, 2, 1, 3),
        master.transpose(0, 2, 1, 3),
    )
    out, scale, newmom, newmaster = pl.pallas_call(
        finish,
        out_shape=(
            jax.ShapeDtypeStruct((blocks * shard, head), BF16),
            jax.ShapeDtypeStruct((1, blocks), F32),
            jax.ShapeDtypeStruct(moved, BF16),
            jax.ShapeDtypeStruct(moved, F32),
        ),
        in_specs=[hbm] * 4,
        out_specs=[hbm] * 4,
        scratch_shapes=[
            pltpu.VMEM((blocks * shard, head), BF16),
            pltpu.VMEM((1, blocks), F32),
            pltpu.VMEM(moved, BF16),
            pltpu.VMEM(moved, F32),
            sem((7,)),
            sem((7,)),
        ],
        compiler_params=pltpu.CompilerParams(vmem_limit_bytes=VMEM),
        name="write_results",
    )(*results)
    return (
        out.reshape(blocks, shard, head),
        scale.reshape(blocks),
        newmom.transpose(0, 2, 1, 3),
        newmaster.transpose(0, 2, 1, 3),
    )


def solution(mesh):
    in_specs = (
        P("dp", None, "mp", None),
        P(),
        P("mp", None, "dp", None),
        P("mp", None, "dp", None),
    )
    out_specs = (P(None, "mp", None), P(), P("mp", None, "dp", None), P("mp", None, "dp", None))
    return jax.shard_map(body, mesh=mesh, in_specs=in_specs, out_specs=out_specs, check_vma=False)
```

```python
import functools
import math

import jax
import jax.numpy as jnp
from jax import lax
from jax.experimental import pallas as pl
from jax.experimental.pallas import tpu as pltpu
from jax.sharding import PartitionSpec as P

D = 7168
ITERS = 5
NEWTON = (3.4445, -4.775, 2.0315)
decay_rate = 0.95
learn_rate = 0.05
weight_decay = 0.1
update_gain = 0.2

MESH = pl.DeviceIdType.MESH
F32 = jnp.float32
BF16 = jnp.bfloat16
VMEM = 63 * 2**20
NEAR = (1, 2, 8, 13, 19, 24, 30, 31)
SIDE = 4


def dot(a, b):
    return jnp.dot(a, b, precision=lax.Precision.HIGHEST, preferred_element_type=F32)


def kernel(n_dp, n_mp, cap, blocks, rows, owners_hbm, grad_hbm, mom_hbm, master_hbm,
           out_hbm, scale_ref, newmom_hbm, newmaster_hbm,
           owners_ref, grad_ref, mom_ref, master_ref, wide, newmom_ref, newmaster_ref,
           rs1_out_a, rs1_out_b, rs1_in_a, rs1_in_b, rs2_out_a, rs2_out_b, rs2_in_a, rs2_in_b,
           z32, z_out, z_in, upd, gram_out, gram_in, gram_all, y_out, y_in, ag_a, ag_b,
           near_sem, in_sem, out_sem, rs1_s, rs1_r, rs2_s, rs2_r, z_s, z_r, g_s, g_r, h_s, h_r, y_s, y_r,
           ag1_s, ag1_r, ag2_s, ag2_r):
    dp, mp = lax.axis_index("dp"), lax.axis_index("mp")
    side = SIDE
    x, y = dp // side, lax.rem(dp, side)
    slots = n_mp * cap
    shard = n_dp * rows
    half = blocks // 2
    few, many = 0, 1
    starts, counts = (8, 0), (rows - 8, 8)
    rs1_out, rs1_in = (rs1_out_a, rs1_out_b), (rs1_in_a, rs1_in_b)
    rs2_out, rs2_in = (rs2_out_a, rs2_out_b), (rs2_in_a, rs2_in_b)
    ag = (ag_a, ag_b)
    first, second = (x, y), (y, x)

    def dp_at(h, f, s):
        return f * side + s if h == 0 else s * side + f

    def ahead(v, k, n):
        return lax.rem(v + k, n)

    def behind(v, k, n):
        return lax.rem(v + n - k, n)

    def remote(src, dst, send, recv, **to):
        return pltpu.make_async_remote_copy(
            src_ref=src, dst_ref=dst, send_sem=send, recv_sem=recv, device_id=to, device_id_type=MESH)

    def all_sent(ref, sem):
        remote(ref, ref, sem, sem, dp=ahead(dp, 1, n_dp)).wait_send()

    def all_here(ref, sem):
        remote(ref, ref, sem, sem, dp=ahead(dp, 1, n_dp)).wait_recv()

    def z_offset(j):
        return n_mp // 2 + ((j + 1) // 2) * (1 - 2 * lax.rem(j, 2))

    loads = [
        pltpu.make_async_copy(src, dst, in_sem.at[i])
        for i, (src, dst) in enumerate((
            (grad_hbm.at[0:half * shard], grad_ref.at[0:half * shard]),
            (grad_hbm.at[half * shard:], grad_ref.at[half * shard:]),
            (owners_hbm, owners_ref), (mom_hbm, mom_ref), (master_hbm, master_ref)))
    ]
    for load in loads:
        load.start()

    barrier = pltpu.get_barrier_semaphore()

    for k in range(1, side):
        for h in range(2):
            f = ahead(first[h], k, side)
            pl.semaphore_signal(barrier, 1, device_id={"dp": dp_at(h, f, second[h])}, device_id_type=MESH)
    for k in NEAR:
        pl.semaphore_signal(barrier, 1, device_id={"mp": ahead(mp, k, n_mp)}, device_id_type=MESH)

    for h in range(2):
        loads[h].wait()

        @pl.loop(0, half)
        def _(i):
            at = pl.ds(pl.multiple_of((h * half + i) * shard, 16), shard)
            wide[at, :] = grad_ref[at, :].astype(F32)

    def pick(q, h, f, dst):
        @pl.loop(0, side)
        def _(s):
            base = h * half * shard + dp_at(h, f, s) * rows + starts[q]
            for r in range(counts[q]):
                dst[s, r] = wide[pl.ds(base + r, half, stride=shard), :].astype(BF16)

    pl.semaphore_wait(barrier, 2 * (side - 1) + len(NEAR))

    def rs1(q, h, f):
        return remote(rs1_out[q].at[h, f], rs1_in[q].at[h, first[h]], rs1_s.at[q, h], rs1_r.at[q, h],
                      dp=dp_at(h, f, second[h]))

    def rs2(q, h, s):
        return remote(rs2_out[q].at[h, s], rs2_in[q].at[h, second[h]], rs2_s.at[q, h], rs2_r.at[q, h],
                      dp=dp_at(h, first[h], s))

    for q in (few, many):
        for k in range(1, side):
            for h in range(2):
                f = ahead(first[h], k, side)
                pick(q, h, f, rs1_out[q].at[h, f])
                rs1(q, h, f).start()
        for h in range(2):
            pick(q, h, first[h], rs1_in[q].at[h, first[h]])

    loads[2].wait()
    lane = lax.broadcasted_iota(jnp.int32, (8, 128), 1)
    owner_row = jnp.full((8, 128), -1, jnp.int32)
    for b in range(blocks):
        owner_row = jnp.where(lane == b, owners_ref[b], owner_row)
    position = jnp.zeros((8, 128), jnp.int32)
    for b in range(blocks):
        position = position + jnp.where((owner_row == owners_ref[b]) & (lane > b), 1, 0)
    slot_row = jnp.where(owner_row >= 0, owner_row * cap + position, -1)[0:1, 0:blocks]
    place = jnp.broadcast_to(slot_row, (slots, blocks)) == lax.broadcasted_iota(jnp.int32, (slots, blocks), 0)
    onehot = jnp.where(place, 1.0, 0.0).astype(F32)
    onehot_t = onehot.T.astype(BF16)
    onehot = onehot.astype(BF16)
    count = jnp.int32(0)
    for b in range(blocks):
        count = count + jnp.where(owners_ref[b] == mp, 1, 0)

    for k in NEAR:
        pl.semaphore_signal(near_sem, 1, device_id={"mp": ahead(mp, k, n_mp)}, device_id_type=MESH)
    z32[...] = jnp.zeros_like(z32)

    def z_copy(j, q, src, dst, s, r):
        to = ahead(mp, z_offset(j), n_mp)
        return remote(src.at[q, to], dst.at[q, mp], s.at[q], r.at[q], mp=to)

    def z_send(q, src, dst, s, r):
        @pl.loop(0, n_mp - 1)
        def _(j):
            z_copy(j, q, src, dst, s, r).start()

        dst[q, mp] = src[q, mp]

    for q in (few, many):
        for h in range(2):
            all_here(rs1_in[q].at[h, 0:side - 1], rs1_r.at[q, h])
            for k in range(1, side + 1):
                s = ahead(second[h], k, side)
                for r in range(counts[q]):
                    total = rs1_in[q][h, 0, s, r].astype(F32)
                    for f in range(1, side):
                        total = total + rs1_in[q][h, f, s, r].astype(F32)
                    if k < side:
                        rs2_out[q][h, s, r] = total.astype(BF16)
                    else:
                        rs2_in[q][h, s, r] = total.astype(BF16)
                if k < side:
                    rs2(q, h, s).start()
        if q == few:
            pl.semaphore_wait(near_sem, len(NEAR))
        for h in range(2):
            all_here(rs2_in[q].at[h, 0:side - 1], rs2_r.at[q, h])
        for r in range(counts[q]):
            both = []
            for h in range(2):
                total = rs2_in[q][h, 0, r].astype(F32)
                for s in range(1, side):
                    total = total + rs2_in[q][h, s, r].astype(F32)
                both.append(total)
            total = jnp.concatenate(both, axis=0).astype(BF16)
            z32[pl.ds(r, slots, stride=8), :] = jnp.dot(onehot, total, preferred_element_type=F32)
        z_out[q] = z32[...].astype(BF16).reshape(n_mp, cap * 8, 128)
        z_send(q, z_out, z_in, z_s, z_r)

    loads[3].wait()
    loads[4].wait()
    parts_of = [[] for _ in range(cap)]
    for q in (few, many):
        all_here(z_in.at[q, 0:n_mp - 1], z_r.at[q])
        z32[...] = z_in[q].reshape(z32.shape).astype(F32)
        for c in range(cap):
            for j in range(counts[q]):
                r = starts[q] + j
                arrived = z32[pl.ds(c * 8 + j, n_mp, stride=cap * 8), :]
                before = mom_ref[c, r]
                after = (decay_rate * before.astype(F32) + arrived).astype(BF16)
                newmom_ref[c, r] = jnp.where(count > c, after, before)
                upd[c, pl.ds(r * n_mp, n_mp), :] = arrived + decay_rate * after.astype(F32)
            u = upd[c, starts[q] * n_mp:(starts[q] + counts[q]) * n_mp, :]
            parts_of[c].append(lax.dot_general(
                u, u, (((0,), (0,)), ((), ())), precision=lax.Precision.HIGHEST, preferred_element_type=F32))

    stores = [pltpu.make_async_copy(newmom_ref, newmom_hbm, out_sem.at[0])]
    stores[0].start()

    piece = 128 // n_dp
    for c in range(cap):
        gram = parts_of[c][0] + parts_of[c][1]
        for d in range(n_dp):
            gram_out[d, c] = gram[d * piece:(d + 1) * piece, :]

    for k in (10, 9, 11, 6, 14, 5, 7, 13, 15, 2, 8, 1, 3, 4, 12):
        to = ahead(dp, k, n_dp)
        remote(gram_out.at[to], gram_in.at[dp], g_s, g_r, dp=to).start()

    gram_in[dp] = gram_out[dp]

    all_here(gram_in.at[0:n_dp - 1], g_r)

    part = gram_in[0]
    for s in range(1, n_dp):
        part = part + gram_in[s]
    gram_all[dp] = part

    for k in (10, 9, 11, 6, 14, 5, 7, 13, 15, 2, 8, 1, 3, 4, 12):
        to = ahead(dp, k, n_dp)
        remote(gram_all.at[dp], gram_all.at[dp], h_s, h_r, dp=to).start()

    all_here(gram_all.at[0:n_dp - 1], h_r)

    eye = lax.broadcasted_iota(jnp.int32, (128, 128), 0) == lax.broadcasted_iota(jnp.int32, (128, 128), 1)
    a0, a1, a2 = NEWTON
    grams, norms = [], []
    for c in range(cap):
        raw = gram_all[:, c].reshape(128, 128)
        norm = jnp.sqrt(jnp.sum(jnp.where(eye, raw, 0.0), axis=(0, 1), keepdims=True)) + 1e-07
        grams.append(raw / (norm * norm))
        norms.append(norm)
    polys = [None] * cap
    for i in range(ITERS):
        mixes = [a1 * g + a2 * dot(g, g) for g in grams]
        if i == 0:
            polys = [jnp.where(eye, a0, 0.0) + m for m in mixes]
        else:
            both = [dot(jnp.concatenate([p, g], axis=0), m) for p, g, m in zip(polys, grams, mixes)]
            polys = [a0 * p + b[0:128] for p, b in zip(polys, both)]
        if i < ITERS - 1:
            products = [b[128:] for b in both] if i else [dot(g, m) for g, m in zip(grams, mixes)]
            halves = [a0 * g + b for g, b in zip(grams, products)]
            grams = [a0 * h + dot(h, m) for h, m in zip(halves, mixes)]
    polys = [p * (-learn_rate * update_gain * math.sqrt(D) / n) for p, n in zip(polys, norms)]

    peaks = [jnp.zeros((n_mp, 128), F32)] * cap
    for q in (many, few):
        for c in range(cap):
            at, size = starts[q] * n_mp, counts[q] * n_mp
            step = dot(upd[c, at:at + size, :], polys[c])
            for j in range(counts[q]):
                r = starts[q] + j
                before = master_ref[c, r]
                after = before * (1.0 - learn_rate * weight_decay) + step[j * n_mp:(j + 1) * n_mp, :]
                newmaster_ref[c, r] = jnp.where(count > c, after, before)
                peaks[c] = jnp.maximum(peaks[c], jnp.abs(after))
                z32[pl.ds(c * 8 + j, n_mp, stride=cap * 8), :] = after
            if q == few:
                peak = jnp.broadcast_to(jnp.max(peaks[c], axis=(0, 1), keepdims=True), (n_mp, 128))
                high = peak.astype(BF16).astype(F32)
                low = peak - high
                left = lax.broadcasted_iota(jnp.int32, (n_mp, 128), 1) < 64
                z32[pl.ds(c * 8 + counts[q], n_mp, stride=cap * 8), :] = jnp.where(left, high, low)
        y_out[q] = z32[...].astype(BF16).reshape(n_mp, cap * 8, 128)
        z_send(q, y_out, y_in, y_s, y_r)

    stores.append(pltpu.make_async_copy(newmaster_ref, newmaster_hbm, out_sem.at[1]))
    stores[1].start()

    def ag1(q, h, k, p):
        return remote(ag[q].at[h, second[h], 0], ag[q].at[h, second[h], k], ag1_s.at[q, h, k], ag1_r.at[q, h, k],
                      dp=dp_at(h, p, second[h]))

    def ag2(q, h, s, p, part):
        at = ag[q].at[h, s, part]
        return remote(at, at, ag2_s.at[q, h, part], ag2_r.at[q, h, part], dp=dp_at(h, first[h], p))

    sent = (counts[0] + 1, counts[1])
    for q in (many, few):
        all_here(y_in.at[q, 0:n_mp - 1], y_r.at[q])
        z32[...] = y_in[q].reshape(z32.shape).astype(F32)
        for r in range(sent[q]):
            v = z32[pl.ds(r, slots, stride=8), :].astype(BF16)
            v = jnp.dot(onehot_t, v, preferred_element_type=F32)
            for h in range(2):
                ag[q][h, second[h], 0, r] = v[h * half:(h + 1) * half, :].astype(BF16)
        for k in range(1, side):
            for h in range(2):
                ag1(q, h, k, ahead(first[h], k, side)).start()
        for k in range(1, side):
            for h in range(2):
                ag2(q, h, second[h], ahead(second[h], k, side), 0).start()
        for c in (1, 3, 2):
            for h in range(2):
                at = ag[q].at[h, second[h], c]
                remote(at, at, ag1_s.at[q, h, c], ag1_r.at[q, h, c], dp=ahead(dp, 1, n_dp)).wait_recv()
                for k in (2, 1, 3):
                    ag2(q, h, second[h], ahead(second[h], k, side), c).start()

    def spread(q, h, s, k):
        f = behind(first[h], k, side)
        base = h * half * shard + dp_at(h, f, s) * rows + starts[q]
        for r in range(counts[q]):
            wide[pl.ds(base + r, half, stride=shard), :] = ag[q][h, s, k, r].astype(F32)

    for q in (many, few):
        for h in range(2):
            for k in range(side):
                spread(q, h, second[h], k)
    for q in (many, few):
        for part in (0, 1, 3, 2):
            for h in range(2):
                all_here(ag[q].at[h, 0:side - 1, part], ag2_r.at[q, h, part])
                for k in range(1, side):
                    s = behind(second[h], k, side)
                    spread(q, h, s, part)

    both = []
    for h in range(2):
        peak = jnp.zeros((half, 128), F32)
        for s in range(side):
            for f in range(side):
                v = ag[few][h, s, f, counts[few]].astype(F32)
                peak = jnp.maximum(peak, v + pltpu.roll(v, 64, 1))
        both.append(peak)
    peak = jnp.concatenate(both, axis=0) + 1e-06
    scale_ref[...] = peak.T[0:1, :]
    z32[0:blocks, :] = 1.0 / peak
    parts = 4
    step = blocks // parts
    for i in range(parts):

        @pl.loop(i * step, i * step + step)
        def _(b):
            at = pl.ds(pl.multiple_of(b * shard, 16), shard)
            grad_ref[at, :] = (wide[at, :] * z32[pl.ds(b, 1), :]).astype(BF16)

        part = pl.ds(i * step * shard, step * shard)
        stores.append(pltpu.make_async_copy(grad_ref.at[part], out_hbm.at[part], out_sem.at[2 + i]))
        stores[-1].start()
    for store in stores:
        store.wait()

    for q in range(2):
        all_sent(z_out.at[q, 0:n_mp - 1], z_s.at[q])
        all_sent(y_out.at[q, 0:n_mp - 1], y_s.at[q])
        for h in range(2):
            all_sent(rs1_out[q].at[h, 0:side - 1], rs1_s.at[q, h])
            all_sent(rs2_out[q].at[h, 0:side - 1], rs2_s.at[q, h])
            for c in range(side):
                if c:
                    all_sent(ag[q].at[h, 0, c], ag1_s.at[q, h, c])
                all_sent(ag[q].at[h, 0:side - 1, c], ag2_s.at[q, h, c])
    all_sent(gram_out.at[0:n_dp - 1], g_s)
    all_sent(gram_all.at[0:n_dp - 1], h_s)


def finish(out_in, scale_in, newmom_in, newmaster_in, out_hbm, scale_hbm, newmom_hbm, newmaster_hbm,
           out_ref, scale_ref, newmom_ref, newmaster_ref, in_sem, out_sem):
    parts = 4
    step = out_ref.shape[0] // parts
    ways = [(scale_in, scale_ref, scale_hbm)]
    for i in range(parts):
        at = pl.ds(i * step, step)
        ways.append((out_in.at[at], out_ref.at[at], out_hbm.at[at]))
    ways += [(newmaster_in, newmaster_ref, newmaster_hbm), (newmom_in, newmom_ref, newmom_hbm)]
    loads = [pltpu.make_async_copy(a, b, in_sem.at[i]) for i, (a, b, _) in enumerate(ways)]
    stores = [pltpu.make_async_copy(b, c, out_sem.at[i]) for i, (_, b, c) in enumerate(ways)]
    for load in loads:
        load.start()
    for load, store in zip(loads, stores):
        load.wait()
        store.start()
    for store in stores:
        store.wait()


def body(gradients, owners, momentum, master):
    n_dp, n_mp = lax.axis_size("dp"), lax.axis_size("mp")
    _, blocks, shard, head = gradients.shape
    cap, _, rows, _ = momentum.shape
    slots = n_mp * cap
    moved = (cap, rows, n_mp, head)
    few, many, half = rows - 8, 8, blocks // 2
    sem = pltpu.SemaphoreType.DMA
    hbm = pl.BlockSpec(memory_space=pltpu.HBM)
    vmem = pl.BlockSpec(memory_space=pltpu.VMEM)
    results = pl.pallas_call(
        functools.partial(kernel, n_dp, n_mp, cap, blocks, rows),
        out_shape=(
            jax.ShapeDtypeStruct((blocks * shard, head), BF16),
            jax.ShapeDtypeStruct((1, blocks), F32),
            jax.ShapeDtypeStruct(moved, BF16),
            jax.ShapeDtypeStruct(moved, F32),
        ),
        in_specs=[hbm] * 4,
        out_specs=(hbm, vmem, hbm, hbm),
        scratch_shapes=[
            pltpu.SMEM((blocks,), jnp.int32),
            pltpu.VMEM((blocks * shard, head), BF16),
            pltpu.VMEM(moved, BF16),
            pltpu.VMEM(moved, F32),
            pltpu.VMEM((blocks * shard, head), F32),
            pltpu.VMEM(moved, BF16),
            pltpu.VMEM(moved, F32),
            *[pltpu.VMEM((2, SIDE, SIDE, n, half, head), BF16) for n in (few, many)],
            *[pltpu.VMEM((2, SIDE, SIDE, n, half, head), BF16) for n in (few, many)],
            *[pltpu.VMEM((2, SIDE, n, half, head), BF16) for n in (few, many)],
            *[pltpu.VMEM((2, SIDE, n, half, head), BF16) for n in (few, many)],
            pltpu.VMEM((slots * 8, head), F32),
            pltpu.VMEM((2, n_mp, cap * 8, head), BF16),
            pltpu.VMEM((2, n_mp, cap * 8, head), BF16),
            pltpu.VMEM((cap, rows * n_mp, head), F32),
            *[pltpu.VMEM((n_dp, cap, head // n_dp, head), F32)] * 3,
            pltpu.VMEM((2, n_mp, cap * 8, head), BF16),
            pltpu.VMEM((2, n_mp, cap * 8, head), BF16),
            *[pltpu.VMEM((2, SIDE, SIDE, n, half, head), BF16) for n in (few + 1, many)],
            pltpu.SemaphoreType.REGULAR,
            sem((5,)),
            sem((6,)),
            *[sem((2, 2))] * 4,
            *[sem((2,))] * 2,
            *[sem(())] * 4,
            *[sem((2,))] * 2,
            *[sem((2, 2, SIDE))] * 4,
        ],
        compiler_params=pltpu.CompilerParams(
            collective_id=0, has_side_effects=True, vmem_limit_bytes=VMEM),
        name="muon_step",
    )(
        owners,
        gradients.reshape(blocks * shard, head),
        momentum.transpose(0, 2, 1, 3),
        master.transpose(0, 2, 1, 3),
    )
    out, scale, newmom, newmaster = pl.pallas_call(
        finish,
        out_shape=(
            jax.ShapeDtypeStruct((blocks * shard, head), BF16),
            jax.ShapeDtypeStruct((1, blocks), F32),
            jax.ShapeDtypeStruct(moved, BF16),
            jax.ShapeDtypeStruct(moved, F32),
        ),
        in_specs=[hbm] * 4,
        out_specs=[hbm] * 4,
        scratch_shapes=[
            pltpu.VMEM((blocks * shard, head), BF16),
            pltpu.VMEM((1, blocks), F32),
            pltpu.VMEM(moved, BF16),
            pltpu.VMEM(moved, F32),
            sem((7,)),
            sem((7,)),
        ],
        compiler_params=pltpu.CompilerParams(vmem_limit_bytes=VMEM),
        name="write_results",
    )(*results)
    return (
        out.reshape(blocks, shard, head),
        scale.reshape(blocks),
        newmom.transpose(0, 2, 1, 3),
        newmaster.transpose(0, 2, 1, 3),
    )


def solution(mesh):
    in_specs = (
        P("dp", None, "mp", None),
        P(),
        P("mp", None, "dp", None),
        P("mp", None, "dp", None),
    )
    out_specs = (P(None, "mp", None), P(), P("mp", None, "dp", None), P("mp", None, "dp", None))
    return jax.shard_map(body, mesh=mesh, in_specs=in_specs, out_specs=out_specs, check_vma=False)
```
